128 devices in a mesh: row: 8 (over z, y_hi), col: 16 (over x, y_lo, core).
Axes of the slice: x: 4, y: 4 (y_hi: 2, y_lo: 2; y = y_hi * 2 + y_lo), z: 4, core: 2. Of those that a mesh axis runs over, the one named last changes fastest.
Arguments:
- amplitudes: bfloat16 [10000, 4096], P('row', 'col'), may hold values from -6 to 6
- integrals: bfloat16 [4096, 16384], P(('row', 'col')), may hold values from -0.09375 to 0.09375
- storage_slot: int32 [4096], P('row'), may hold values from 0 to 4095, as said below
Outputs:
- ladder: float32 [10000, 16384], P(None, ('col', 'row'))
The draws below stay inside these ranges and needn't reach their ends.
Inputs may be any that keep to these rules, and one draw needn't show every extreme that they name: storage_slot is a permutation of 0 to 4095 that keeps every index k within its own aligned block of 4096 // 8 indices.
All inputs are finite; a program needn't handle non-finite values.
Results may differ from the reference program's by a relative error of at most 0.0003.
Values may be sent and summed in bfloat16 or wider, within the bound.
A program may use at most 64 MiB of HBM per device.

```python
import jax
import jax.numpy as jnp

PAIRS = 10000
K = 4096
N = 16384
N_ROW = 8


def draw_storage_slot(key, part):
    key = jax.random.fold_in(key, 7)
    block_rows = K // N_ROW
    block_keys = jax.random.split(key, N_ROW)
    shuffled = jax.vmap(lambda sub_key: jax.random.permutation(sub_key, block_rows))(block_keys)
    offsets = jnp.arange(N_ROW, dtype=jnp.int32) * block_rows
    return (shuffled.astype(jnp.int32) + offsets[:, None]).reshape(K).astype(jnp.int32)


def levels(stream_key, dims, shards, smallest, high):
    def one(axis_at, blocks):
        heights = jax.random.uniform(jax.random.fold_in(jax.random.fold_in(stream_key, 6), axis_at), (blocks,), jnp.float32, smallest / len(shards), high / len(shards))
        return jnp.repeat(jnp.exp(heights), dims[axis_at] // blocks).reshape((-1,) + (1,) * (len(dims) - axis_at - 1))

    loudness = one(*shards[0])
    for cut in shards[1:]:
        loudness = loudness * one(*cut)
    return loudness


def noise(key, dims, spread, limit, cuts=(), held_as=jnp.bfloat16):
    gain = levels(key, dims, cuts, -0.22, 0.18) if cuts else 1.0
    array = jax.random.normal(key, dims, jnp.float32) * spread * gain
    return jnp.minimum(jnp.maximum(array, -limit), limit).astype(held_as)


def setup_inputs(seed: int = 0) -> dict:
    streams_of = jax.random.split(jax.random.key(seed), 4)
    return {
        "amplitudes": noise(streams_of[0], (PAIRS, K), 1.0, 6.0, ((0, 8), (1, 16))),
        "integrals": noise(streams_of[1], (K, N), K ** -0.5, 0.09375, ((0, 128),)),
        "storage_slot": draw_storage_slot(jax.random.fold_in(streams_of[3], 71), 0),
    }


def reference(amplitudes, integrals, storage_slot):
    ordered = jnp.take(integrals, storage_slot.astype(jnp.int32), axis=0)
    return jnp.dot(amplitudes, ordered, preferred_element_type=jnp.float32)
```

```python
import functools

import jax
import jax.numpy as jnp
from jax import lax
from jax.experimental import pallas as pl
from jax.experimental.pallas import tpu as pltpu
from jax.sharding import PartitionSpec as P

MESH = pl.DeviceIdType.MESH
T = 128
TILES = 5
HALF = T * TILES
LIFT = 2.0**40
TOP = 32767.0


def device(x, y, z, k):
    return (z * 2 + y // 2, (x * 2 + y % 2) * 2 + k)


def wait(ref, sem):
    pltpu.make_async_copy(ref, ref, sem).wait()


def ladder_kernel(
    a_ref, i_ref, slot_ref, q_ref, m_ref,
    apad, lhs, onehot, slots, ipack, amp, ints, codes, tops,
    slot_send, slot_recv, half_send, half_recv, own_sem,
    plane_send, plane_recv, line_send, line_recv, pair_send, pair_recv,
    amp_send, amp_recv, out_send, out_recv, top_send, top_recv,
):
    row, col = lax.axis_index("row"), lax.axis_index("col")
    x, y, z, k = col // 4, (row % 2) * 2 + (col // 2) % 2, row // 2, col % 2
    block = col // 2
    me = (row % 2) * 8 + block

    def chip_of(p):
        return (p % 8) // 2, (p // 8) * 2 + p % 2

    def place(px, py):
        return (py // 2) * 8 + px * 2 + py % 2

    barrier = pltpu.get_barrier_semaphore()

    def greet(d):
        pl.semaphore_signal(barrier, inc=1, device_id=d, device_id_type=MESH)

    for d in range(1, 16):
        px, py = chip_of(me ^ d)
        greet(device(px, py, z, k))
    for d in range(1, 4):
        for c in range(2):
            greet(device(x, y, (z + d) % 4, c))
    greet(device(x, y, z, 1 - k))
    mirrored = row != block

    @pl.when(mirrored)
    def _():
        greet((block, 2 * row + k))

    def pack(p, _):
        px, py = chip_of(p)
        base = (px * 2 + py % 2) * 16 + py // 2
        for zz in range(4):
            for c in range(2):
                at = pl.multiple_of((base + c * 8 + zz * 2) * 128, 128)
                ipack[p, :, (zz * 2 + c) * 128 : (zz * 2 + c + 1) * 128] = i_ref[:, pl.ds(at, 128)]
        return _

    lax.fori_loop(0, 16, pack, None)
    rows = a_ref.shape[0]
    low = rows // 16 * 16
    apad[low:, :] = jnp.zeros((2 * HALF - low, 256), jnp.bfloat16)
    apad[0:rows, :] = a_ref[...]

    def ints_row(zs, p):
        return pl.multiple_of(((zs * 2 + p // 8) * 2 + k) * 256 + (p % 8) * 32, 32)

    mine = pl.ds(ints_row(z, me), 32)
    ints[mine, :] = ipack[me]

    pl.semaphore_wait(barrier, 22 + mirrored.astype(jnp.int32))

    def slot_copy():
        return pltpu.make_async_remote_copy(
            slot_ref, slots, slot_send, slot_recv, device_id=(block, 2 * row + k), device_id_type=MESH
        )

    half_copy = pltpu.make_async_remote_copy(
        apad.at[pl.ds(pl.multiple_of((1 - k) * HALF, HALF), HALF)],
        lhs.at[:, pl.ds(pl.multiple_of(k * 256, 256), 256)],
        half_send, half_recv, device_id=device(x, y, z, 1 - k), device_id_type=MESH,
    )

    @pl.when(mirrored)
    def _():
        slot_copy().start()

    half_copy.start()

    def line_copy(zs, p, to):
        part = ints.at[pl.ds(ints_row(zs, p), 32)]
        pltpu.make_async_remote_copy(
            part, part, line_send, line_recv.at[zs * 16 + p], device_id=device(x, y, to, k), device_id_type=MESH
        ).start()

    def line_wait(zs, p):
        wait(ints.at[pl.ds(ints_row(zs, p), 32)], line_recv.at[zs * 16 + p])

    up, down, far = (z + 1) % 4, (z + 3) % 4, (z + 2) % 4

    def plane_out(d, _):
        p = me ^ d
        px, py = chip_of(p)
        pltpu.make_async_remote_copy(
            ipack.at[p], ints.at[mine], plane_send, plane_recv.at[me],
            device_id=device(px, py, z, k), device_id_type=MESH,
        ).start()
        return _

    lax.fori_loop(1, 16, plane_out, None)
    line_copy(z, me, up)
    line_copy(z, me, down)

    own = pltpu.make_async_copy(
        apad.at[pl.ds(pl.multiple_of(k * HALF, HALF), HALF)],
        lhs.at[:, pl.ds(pl.multiple_of(k * 256, 256), 256)],
        own_sem,
    )
    own.start()

    @pl.when(mirrored)
    def _():
        slot_copy().wait()

    @pl.when(jnp.logical_not(mirrored))
    def _():
        slots[...] = slot_ref[...]

    def mark(s, _):
        at = lax.broadcasted_iota(jnp.int32, (64, 512), 0) + s * 64
        stored = ((at % 256) // 32) * 64 + (at // 256) * 32 + at % 32
        hit = (slots[0:1, :] - block * 512) == stored
        onehot[pl.ds(pl.multiple_of(s * 64, 64), 64), :] = jnp.where(hit, 1.0, 0.0).astype(jnp.bfloat16)
        return _

    lax.fori_loop(0, 8, mark, None)
    half_copy.wait()
    own.wait()

    def amp_rows(t, yhi):
        return pl.ds(pl.multiple_of((t * 2 + yhi) * T, T), T)

    def order(t, _):
        part = lax.dot_general(
            lhs[pl.ds(pl.multiple_of(t * T, T), T), :], onehot[...], (((1,), (1,)), ((), ())),
            preferred_element_type=jnp.float32,
        )
        amp[amp_rows(t, row % 2), pl.ds(pl.multiple_of(block * 512, 512), 512)] = part.astype(jnp.bfloat16)
        return _

    lax.fori_loop(0, TILES, order, None)

    def piece(t, px, py, c):
        return amp.at[
            amp_rows(t, py // 2),
            pl.ds(pl.multiple_of(((px * 2 + py % 2) * 2 + c) * 256, 256), 256),
        ]

    def at(u, v, c):
        fx, fy = (u, v) if c == 0 else (v, u)
        return (x + fx) % 4, (y + fy) % 4

    def amp_sem(t, px, py, c):
        return amp_recv.at[(t * 16 + place(px, py)) * 2 + c]

    def send(t, src, c, to):
        part = piece(t, *src, c)
        pltpu.make_async_remote_copy(
            part, part, amp_send.at[t], amp_sem(t, *src, c), device_id=device(*to, z, k), device_id_type=MESH
        ).start()

    def arrive(t, src, c):
        wait(piece(t, *src, c), amp_sem(t, *src, c))

    def when(cond):
        return pl.when(cond) if not isinstance(cond, bool) else (lambda f: f() if cond else None)

    def first(t):
        for c in range(2):
            for s in (1, 3):
                send(t, at(0, 0, c), c, at(s, 0, c))

    def spread(t, src, c):
        for s in (1, 3):
            send(t, src, c, at(0, s, c))

    def second(t):
        for c in range(2):
            spread(t, at(0, 0, c), c)
            for s in (1, 3):
                arrive(t, at(s, 0, c), c)
                spread(t, at(s, 0, c), c)
            go = 1 + 2 * ((t + c) % 2)
            send(t, at(4 - go, 0, c), c, at(go, 0, c))

    def third(t):
        for c in range(2):
            arrive(t, at(2, 0, c), c)
            spread(t, at(2, 0, c), c)

    def fourth(t):
        for u in (0, 1, 3, 2):
            for c in range(2):
                go = 1 if u % 2 == 0 else 3
                arrive(t, at(u, 4 - go, c), c)
                send(t, at(u, 4 - go, c), c, at(0, go, c))

    def fifth(t):
        for u in range(4):
            for c in range(2):
                go = 1 if u % 2 == 0 else 3
                arrive(t, at(u, go, c), c)
                arrive(t, at(u, 2, c), c)

    def turn(i):
        @pl.when(i + 2 < TILES)
        def _():
            first(i + 2)

        @pl.when(i + 1 < TILES)
        def _():
            second(i + 1)

        @pl.when(i >= 0)
        def _():
            fourth(i)

        @pl.when(i + 1 < TILES)
        def _():
            third(i + 1)

    first(0)

    def plane_in(d, _):
        p = me ^ d
        wait(ints.at[pl.ds(ints_row(z, p), 32)], plane_recv.at[p])
        line_copy(z, p, up)
        line_copy(z, p, down)
        return _

    lax.fori_loop(1, 16, plane_in, None)

    def pair_part(zs, yhi, core):
        return ints.at[pl.ds(pl.multiple_of(((zs * 2 + yhi) * 2 + core) * 256, 256), 256)]

    def pair_out(zs):
        for yhi in range(2):
            pltpu.make_async_remote_copy(
                pair_part(zs, yhi, k), pair_part(zs, yhi, k), pair_send, pair_recv.at[zs * 2 + yhi],
                device_id=device(x, y, z, 1 - k), device_id_type=MESH,
            ).start()

    pair_out(z)

    def relay(p):
        src, to = (z + 3 + 2 * (p % 2)) % 4, (z + 1 + 2 * (p % 2)) % 4
        line_wait(src, p)
        line_copy(src, p, to)

    def opening(step, _):
        turn(step - 1)

        @pl.when((step == 1) | (step == 2))
        def _():
            def one(j, _):
                relay(me ^ ((step - 1) * 8 + j))
                return _

            lax.fori_loop(0, 8, one, None)

        return _

    lax.fori_loop(0, 4, opening, None)

    def rest(p, _):
        line_wait((z + 1 + 2 * (p % 2)) % 4, p)
        return _

    lax.fori_loop(0, 16, rest, None)
    pair_out(up)
    pair_out(down)

    def last(p, _):
        line_wait(far, p)
        return _

    lax.fori_loop(0, 16, last, None)
    pair_out(far)
    for zs in range(4):
        for yhi in range(2):
            wait(pair_part(zs, yhi, 1 - k), pair_recv.at[zs * 2 + yhi])

    def multiply(t):
        def one(n, _):
            to = (z + 2 + 3 * n) % 4
            total = jnp.dot(
                amp[pl.ds(pl.multiple_of(t * 2 * T, 2 * T), 2 * T), :],
                ints[:, pl.ds(pl.multiple_of(to * 256, 256), 256)],
                preferred_element_type=jnp.float32,
            )
            for c in range(2):
                for yhi in range(2):
                    part = total[yhi * T : (yhi + 1) * T, c * 128 : (c + 1) * 128]
                    top = jnp.max(jnp.abs(part), axis=0, keepdims=True)
                    scale = TOP / jnp.maximum(top * LIFT, 1e-28)
                    code = jnp.round((part * LIFT) * scale)
                    codes[t, to * 2 + c, yhi] = code.astype(jnp.int32).astype(jnp.int16)
                    tops[to * 2 + c, pl.ds(yhi * 8 + t, 1), :] = top
                src = codes.at[t, to * 2 + c]
                dst = q_ref.at[z, :, k * TILES + t]
                here = (to == z) & (k == c)

                @pl.when(here)
                def _():
                    pltpu.make_async_copy(src, dst, out_recv.at[z * 2 + k]).start()

                @pl.when(jnp.logical_not(here))
                def _():
                    pltpu.make_async_remote_copy(
                        src, dst, out_send.at[t], out_recv.at[z * 2 + k],
                        device_id=device(x, y, to, c), device_id_type=MESH,
                    ).start()

            return _

        lax.fori_loop(0, 4, one, None)

    tops[...] = jnp.zeros_like(tops)

    def closing(t, _):
        fifth(t)
        multiply(t)

        @pl.when((t >= 1) & (t <= 2))
        def _():
            turn(t + 2)

        return _

    lax.fori_loop(0, TILES, closing, None)

    for d in range(4):
        for c in range(2):
            to = (z + d) % 4
            src, dst = tops.at[to * 2 + c], m_ref.at[z, k]
            if d:
                pltpu.make_async_remote_copy(
                    src, dst, top_send.at[d * 2 + c], top_recv.at[z * 2 + k],
                    device_id=device(x, y, to, c), device_id_type=MESH,
                ).start()
    other = pltpu.make_async_remote_copy(
        tops.at[z * 2 + 1 - k], m_ref.at[z, k], top_send.at[0], top_recv.at[z * 2 + k],
        device_id=device(x, y, z, 1 - k), device_id_type=MESH,
    )
    other.start()
    pltpu.make_async_copy(tops.at[z * 2 + k], m_ref.at[z, k], top_recv.at[z * 2 + k]).start()

    wait(ipack.at[0:15], plane_send)
    wait(ints.at[0 : 48 * 32], line_send)
    wait(ints.at[0 : 8 * 256], pair_send)
    for t in range(TILES):
        wait(amp.at[0 : 30 * T * 256 // 4096], amp_send.at[t])
        wait(codes.at[t, 0:7], out_send.at[t])
    wait(tops.at[0], top_send.at[0])
    for d in range(1, 4):
        for c in range(2):
            wait(tops.at[0], top_send.at[d * 2 + c])
    for zs in range(4):
        for c in range(2):
            wait(q_ref.at[zs, :, c * TILES : (c + 1) * TILES], out_recv.at[zs * 2 + c])
            wait(m_ref.at[zs, c], top_recv.at[zs * 2 + c])


def decode_kernel(block_rows, q_ref, m_ref, o_ref):
    for r in range(4):
        for n in range(2 * TILES):
            rows = min(T, block_rows - n * T)
            if rows <= 0:
                continue
            code = q_ref[r, n * T : (n + 1) * T, :].astype(jnp.int32).astype(jnp.float32)
            at = (r % 2) * 8 + n % TILES
            top = m_ref[r // 2, n // TILES, at : at + 1, :]
            value = (code * (1.0 / TOP)) * top
            o_ref[r * block_rows + n * T : r * block_rows + n * T + rows, :] = value[0:rows]


def shards(amplitudes, integrals, storage_slot):
    dma = pltpu.SemaphoreType.DMA
    bf16 = jnp.bfloat16
    vmem = pl.BlockSpec(memory_space=pltpu.VMEM)
    hbm = pl.BlockSpec(memory_space=pl.ANY)
    codes, tops = pl.pallas_call(
        ladder_kernel,
        out_shape=(
            jax.ShapeDtypeStruct((4, 2, 2 * TILES, T, 128), jnp.int16),
            jax.ShapeDtypeStruct((4, 2, 16, 128), jnp.float32),
        ),
        in_specs=[vmem] * 3,
        out_specs=(hbm, hbm),
        scratch_shapes=[
            pltpu.VMEM((2 * HALF, 256), bf16),
            pltpu.VMEM((HALF, 512), bf16),
            pltpu.VMEM((512, 512), bf16),
            pltpu.VMEM((8, 512), jnp.int32),
            pltpu.VMEM((16, 32, 1024), bf16),
            pltpu.VMEM((2 * HALF, 4096), bf16),
            pltpu.VMEM((4096, 1024), bf16),
            pltpu.VMEM((TILES, 8, 2, T, 128), jnp.int16),
            pltpu.VMEM((8, 16, 128), jnp.float32),
            dma, dma, dma, dma, dma,
            dma, dma((16,)), dma, dma((64,)), dma, dma((8,)),
            dma((TILES,)), dma((TILES * 32,)), dma((TILES,)), dma((8,)), dma((8,)), dma((8,)),
        ],
        compiler_params=pltpu.CompilerParams(
            collective_id=0, has_side_effects=True, vmem_limit_bytes=56 * 2**20
        ),
    )(amplitudes, integrals, jnp.broadcast_to(storage_slot[None, :], (8, 512)))
    rows = amplitudes.shape[0]
    return pl.pallas_call(
        functools.partial(decode_kernel, rows),
        grid=(2,),
        out_shape=jax.ShapeDtypeStruct((8 * rows, 128), jnp.float32),
        in_specs=[
            pl.BlockSpec((4, 2 * HALF, 128), lambda g: (g, 0, 0)),
            pl.BlockSpec((2, 2, 16, 128), lambda g: (g, 0, 0, 0)),
        ],
        out_specs=pl.BlockSpec((4 * rows, 128), lambda g: (g, 0)),
        compiler_params=pltpu.CompilerParams(vmem_limit_bytes=32 * 2**20),
    )(codes.reshape(8, 2 * HALF, 128), tops)


def solution(mesh):
    in_specs = (P("row", "col"), P(("row", "col"), None), P("row"))
    out_specs = P(None, ("col", "row"))
    return jax.shard_map(shards, mesh=mesh, in_specs=in_specs, out_specs=out_specs, check_vma=False)
```

```python
import functools

import jax
import jax.numpy as jnp
from jax import lax
from jax.experimental import pallas as pl
from jax.experimental.pallas import tpu as pltpu
from jax.sharding import PartitionSpec as P

MESH = pl.DeviceIdType.MESH
T = 128
TILES = 5
HALF = T * TILES
LIFT = 2.0**40
TOP = 32767.0
STEPS = (
    (1, 0), (3, 0), (0, 1), (0, 3), (1, 1), (3, 3), (1, 3), (3, 1),
    (2, 0), (0, 2), (2, 1), (2, 3), (1, 2), (3, 2), (2, 2),
)


def device(x, y, z, k):
    return (z * 2 + y // 2, (x * 2 + y % 2) * 2 + k)


def wait(ref, sem):
    pltpu.make_async_copy(ref, ref, sem).wait()


def ladder_kernel(
    a_ref, i_ref, slot_ref, q_ref, m_ref,
    apad, lhs, onehot, slots, ipack, amp, ints, codes, tops,
    slot_send, slot_recv, half_send, half_recv, own_sem,
    plane_send, plane_recv, line_send, line_recv, pair_send, pair_recv,
    amp_send, amp_recv, out_send, out_recv, top_send, top_recv,
):
    row, col = lax.axis_index("row"), lax.axis_index("col")
    x, y, z, k = col // 4, (row % 2) * 2 + (col // 2) % 2, row // 2, col % 2
    block = col // 2
    me = (row % 2) * 8 + block

    def chip_of(p):
        return (p % 8) // 2, (p // 8) * 2 + p % 2

    def place(px, py):
        return (py // 2) * 8 + px * 2 + py % 2

    barrier = pltpu.get_barrier_semaphore()

    def greet(d):
        pl.semaphore_signal(barrier, inc=1, device_id=d, device_id_type=MESH)

    for d in range(1, 16):
        px, py = chip_of(me ^ d)
        greet(device(px, py, z, k))
    for d in range(1, 4):
        for c in range(2):
            greet(device(x, y, (z + d) % 4, c))
    greet(device(x, y, z, 1 - k))
    mirrored = row != block

    @pl.when(mirrored)
    def _():
        greet((block, 2 * row + k))

    def pack(p, _):
        px, py = chip_of(p)
        base = (px * 2 + py % 2) * 16 + py // 2
        for zz in range(4):
            for c in range(2):
                at = pl.multiple_of((base + c * 8 + zz * 2) * 128, 128)
                ipack[p, :, (zz * 2 + c) * 128 : (zz * 2 + c + 1) * 128] = i_ref[:, pl.ds(at, 128)]
        return _

    lax.fori_loop(0, 16, pack, None)
    rows = a_ref.shape[0]
    low = rows // 16 * 16
    apad[low:, :] = jnp.zeros((2 * HALF - low, 256), jnp.bfloat16)
    apad[0:rows, :] = a_ref[...]

    def ints_row(zs, p):
        return pl.multiple_of(((zs * 2 + p // 8) * 2 + k) * 256 + (p % 8) * 32, 32)

    mine = pl.ds(ints_row(z, me), 32)
    ints[mine, :] = ipack[me]

    pl.semaphore_wait(barrier, 22 + mirrored.astype(jnp.int32))

    def slot_copy():
        return pltpu.make_async_remote_copy(
            slot_ref, slots, slot_send, slot_recv, device_id=(block, 2 * row + k), device_id_type=MESH
        )

    half_copy = pltpu.make_async_remote_copy(
        apad.at[pl.ds(pl.multiple_of((1 - k) * HALF, HALF), HALF)],
        lhs.at[:, pl.ds(pl.multiple_of(k * 256, 256), 256)],
        half_send, half_recv, device_id=device(x, y, z, 1 - k), device_id_type=MESH,
    )

    @pl.when(mirrored)
    def _():
        slot_copy().start()

    half_copy.start()

    def line_copy(zs, p, to):
        part = ints.at[pl.ds(ints_row(zs, p), 32)]
        pltpu.make_async_remote_copy(
            part, part, line_send, line_recv.at[zs * 16 + p], device_id=device(x, y, to, k), device_id_type=MESH
        ).start()

    def line_wait(zs, p):
        wait(ints.at[pl.ds(ints_row(zs, p), 32)], line_recv.at[zs * 16 + p])

    up, down, far = (z + 1) % 4, (z + 3) % 4, (z + 2) % 4

    def plane_out(steps):
        for dx, dy in steps:
            px, py = (x + dx) % 4, (y + dy) % 4
            pltpu.make_async_remote_copy(
                ipack.at[place(px, py)], ints.at[mine], plane_send, plane_recv.at[me],
                device_id=device(px, py, z, k), device_id_type=MESH,
            ).start()

    plane_out(STEPS[:8])
    line_copy(z, me, up)
    line_copy(z, me, down)

    own = pltpu.make_async_copy(
        apad.at[pl.ds(pl.multiple_of(k * HALF, HALF), HALF)],
        lhs.at[:, pl.ds(pl.multiple_of(k * 256, 256), 256)],
        own_sem,
    )
    own.start()

    @pl.when(mirrored)
    def _():
        slot_copy().wait()

    @pl.when(jnp.logical_not(mirrored))
    def _():
        slots[...] = slot_ref[...]

    def mark(s, _):
        at = lax.broadcasted_iota(jnp.int32, (64, 512), 0) + s * 64
        stored = ((at % 256) // 32) * 64 + (at // 256) * 32 + at % 32
        hit = (slots[0:1, :] - block * 512) == stored
        onehot[pl.ds(pl.multiple_of(s * 64, 64), 64), :] = jnp.where(hit, 1.0, 0.0).astype(jnp.bfloat16)
        return _

    lax.fori_loop(0, 8, mark, None)
    half_copy.wait()
    own.wait()

    def amp_rows(t, yhi):
        return pl.ds(pl.multiple_of((t * 2 + yhi) * T, T), T)

    def order(t, _):
        part = lax.dot_general(
            lhs[pl.ds(pl.multiple_of(t * T, T), T), :], onehot[...], (((1,), (1,)), ((), ())),
            preferred_element_type=jnp.float32,
        )
        amp[amp_rows(t, row % 2), pl.ds(pl.multiple_of(block * 512, 512), 512)] = part.astype(jnp.bfloat16)
        return _

    lax.fori_loop(0, TILES, order, None)

    def piece(t, px, py, c):
        return amp.at[
            amp_rows(t, py // 2),
            pl.ds(pl.multiple_of(((px * 2 + py % 2) * 2 + c) * 256, 256), 256),
        ]

    def at(u, v, c):
        fx, fy = (u, v) if c == 0 else (v, u)
        return (x + fx) % 4, (y + fy) % 4

    def amp_sem(t, px, py, c):
        return amp_recv.at[(t * 16 + place(px, py)) * 2 + c]

    def send(t, src, c, to):
        part = piece(t, *src, c)
        pltpu.make_async_remote_copy(
            part, part, amp_send.at[t], amp_sem(t, *src, c), device_id=device(*to, z, k), device_id_type=MESH
        ).start()

    def arrive(t, src, c):
        wait(piece(t, *src, c), amp_sem(t, *src, c))

    def first(t):
        for c in range(2):
            for s in (1, 3):
                send(t, at(0, 0, c), c, at(s, 0, c))

    def spread(t, src, c):
        for s in (1, 3):
            send(t, src, c, at(0, s, c))

    def second(t):
        for c in range(2):
            spread(t, at(0, 0, c), c)
            for s in (1, 3):
                arrive(t, at(s, 0, c), c)
                spread(t, at(s, 0, c), c)
            go = 1 + 2 * ((t + c) % 2)
            send(t, at(4 - go, 0, c), c, at(go, 0, c))

    def third(t):
        for c in range(2):
            arrive(t, at(2, 0, c), c)
            spread(t, at(2, 0, c), c)

    def fourth(t):
        for u in (0, 1, 3, 2):
            for c in range(2):
                go = 1 if u % 2 == 0 else 3
                arrive(t, at(u, 4 - go, c), c)
                send(t, at(u, 4 - go, c), c, at(0, go, c))

    def fifth(t):
        for u in range(4):
            for c in range(2):
                go = 1 if u % 2 == 0 else 3
                arrive(t, at(u, go, c), c)
                arrive(t, at(u, 2, c), c)

    sources = [me] + [place((x + 4 - dx) % 4, (y + 4 - dy) % 4) for dx, dy in STEPS]

    def plane_in(parts):
        for p in parts:
            wait(ints.at[pl.ds(ints_row(z, p), 32)], plane_recv.at[p])
            line_copy(z, p, up)
            line_copy(z, p, down)

    plane_out(STEPS[8:])
    first(0)
    first(1)
    plane_in(sources[1:12])
    second(0)
    plane_in(sources[12:])
    third(0)

    def pair_part(zs, yhi, core):
        return ints.at[pl.ds(pl.multiple_of(((zs * 2 + yhi) * 2 + core) * 256, 256), 256)]

    def pair_out(zs):
        for yhi in range(2):
            pltpu.make_async_remote_copy(
                pair_part(zs, yhi, k), pair_part(zs, yhi, k), pair_send, pair_recv.at[zs * 2 + yhi],
                device_id=device(x, y, z, 1 - k), device_id_type=MESH,
            ).start()

    pair_out(z)

    def relay(p):
        src, to = (z + 3 + 2 * (p % 2)) % 4, (z + 1 + 2 * (p % 2)) % 4
        line_wait(src, p)
        line_copy(src, p, to)

    def relays(parts):
        for p in parts:
            relay(p)

    relays(sources[0:4])
    first(2)
    second(1)
    fourth(0)
    third(1)
    relays(sources[4:10])
    first(3)
    second(2)
    relays(sources[10:])
    fourth(1)
    third(2)

    def rest(p, _):
        line_wait((z + 1 + 2 * (p % 2)) % 4, p)
        return _

    lax.fori_loop(0, 16, rest, None)
    pair_out(up)
    pair_out(down)
    first(4)
    second(3)

    def last(p, _):
        line_wait(far, p)
        return _

    lax.fori_loop(0, 16, last, None)
    pair_out(far)
    for zs in range(4):
        for yhi in range(2):
            wait(pair_part(zs, yhi, 1 - k), pair_recv.at[zs * 2 + yhi])

    def multiply(t):
        def one(n, _):
            to = (z + 2 + 3 * n) % 4
            total = jnp.dot(
                amp[pl.ds(pl.multiple_of(t * 2 * T, 2 * T), 2 * T), :],
                ints[:, pl.ds(pl.multiple_of(to * 256, 256), 256)],
                preferred_element_type=jnp.float32,
            )
            for c in range(2):
                for yhi in range(2):
                    part = total[yhi * T : (yhi + 1) * T, c * 128 : (c + 1) * 128]
                    top = jnp.max(jnp.abs(part), axis=0, keepdims=True)
                    scale = TOP / jnp.maximum(top * LIFT, 1e-28)
                    code = jnp.round((part * LIFT) * scale)
                    codes[t, to * 2 + c, yhi] = code.astype(jnp.int32).astype(jnp.int16)
                    tops[to * 2 + c, pl.ds(yhi * 8 + t, 1), :] = top
                src = codes.at[t, to * 2 + c]
                dst = q_ref.at[z, :, k * TILES + t]
                here = (to == z) & (k == c)

                @pl.when(here)
                def _():
                    pltpu.make_async_copy(src, dst, out_recv.at[z * 2 + k]).start()

                @pl.when(jnp.logical_not(here))
                def _():
                    pltpu.make_async_remote_copy(
                        src, dst, out_send.at[t], out_recv.at[z * 2 + k],
                        device_id=device(x, y, to, c), device_id_type=MESH,
                    ).start()

            return _

        lax.fori_loop(0, 4, one, None)

    tops[...] = jnp.zeros_like(tops)

    def closing(t, _):
        fifth(t)
        multiply(t)

        @pl.when(t == 0)
        def _():
            fourth(2)
            third(3)

        @pl.when(t == 1)
        def _():
            second(4)
            fourth(3)
            third(4)

        @pl.when(t == 2)
        def _():
            fourth(4)

        return _

    lax.fori_loop(0, TILES, closing, None)

    for d in range(4):
        for c in range(2):
            to = (z + d) % 4
            src, dst = tops.at[to * 2 + c], m_ref.at[z, k]
            if d:
                pltpu.make_async_remote_copy(
                    src, dst, top_send.at[d * 2 + c], top_recv.at[z * 2 + k],
                    device_id=device(x, y, to, c), device_id_type=MESH,
                ).start()
    other = pltpu.make_async_remote_copy(
        tops.at[z * 2 + 1 - k], m_ref.at[z, k], top_send.at[0], top_recv.at[z * 2 + k],
        device_id=device(x, y, z, 1 - k), device_id_type=MESH,
    )
    other.start()
    pltpu.make_async_copy(tops.at[z * 2 + k], m_ref.at[z, k], top_recv.at[z * 2 + k]).start()

    wait(ipack.at[0:15], plane_send)
    wait(ints.at[0 : 48 * 32], line_send)
    wait(ints.at[0 : 8 * 256], pair_send)
    for t in range(TILES):
        wait(amp.at[0 : 30 * T * 256 // 4096], amp_send.at[t])
        wait(codes.at[t, 0:7], out_send.at[t])
    wait(tops.at[0], top_send.at[0])
    for d in range(1, 4):
        for c in range(2):
            wait(tops.at[0], top_send.at[d * 2 + c])
    for zs in range(4):
        for c in range(2):
            wait(q_ref.at[zs, :, c * TILES : (c + 1) * TILES], out_recv.at[zs * 2 + c])
            wait(m_ref.at[zs, c], top_recv.at[zs * 2 + c])


def decode_kernel(block_rows, q_ref, m_ref, o_ref):
    for r in range(4):
        for n in range(2 * TILES):
            rows = min(T, block_rows - n * T)
            if rows <= 0:
                continue
            code = q_ref[r, n * T : (n + 1) * T, :].astype(jnp.int32).astype(jnp.float32)
            at = (r % 2) * 8 + n % TILES
            top = m_ref[r // 2, n // TILES, at : at + 1, :]
            value = (code * (1.0 / TOP)) * top
            o_ref[r * block_rows + n * T : r * block_rows + n * T + rows, :] = value[0:rows]


def shards(amplitudes, integrals, storage_slot):
    dma = pltpu.SemaphoreType.DMA
    bf16 = jnp.bfloat16
    vmem = pl.BlockSpec(memory_space=pltpu.VMEM)
    hbm = pl.BlockSpec(memory_space=pl.ANY)
    codes, tops = pl.pallas_call(
        ladder_kernel,
        out_shape=(
            jax.ShapeDtypeStruct((4, 2, 2 * TILES, T, 128), jnp.int16),
            jax.ShapeDtypeStruct((4, 2, 16, 128), jnp.float32),
        ),
        in_specs=[vmem] * 3,
        out_specs=(hbm, hbm),
        scratch_shapes=[
            pltpu.VMEM((2 * HALF, 256), bf16),
            pltpu.VMEM((HALF, 512), bf16),
            pltpu.VMEM((512, 512), bf16),
            pltpu.VMEM((1, 512), jnp.int32),
            pltpu.VMEM((16, 32, 1024), bf16),
            pltpu.VMEM((2 * HALF, 4096), bf16),
            pltpu.VMEM((4096, 1024), bf16),
            pltpu.VMEM((TILES, 8, 2, T, 128), jnp.int16),
            pltpu.VMEM((8, 16, 128), jnp.float32),
            dma, dma, dma, dma, dma,
            dma, dma((16,)), dma, dma((64,)), dma, dma((8,)),
            dma((TILES,)), dma((TILES * 32,)), dma((TILES,)), dma((8,)), dma((8,)), dma((8,)),
        ],
        compiler_params=pltpu.CompilerParams(
            collective_id=0, has_side_effects=True, vmem_limit_bytes=56 * 2**20
        ),
    )(amplitudes, integrals, storage_slot.reshape(1, 512))
    rows = amplitudes.shape[0]
    return pl.pallas_call(
        functools.partial(decode_kernel, rows),
        grid=(2,),
        out_shape=jax.ShapeDtypeStruct((8 * rows, 128), jnp.float32),
        in_specs=[
            pl.BlockSpec((4, 2 * HALF, 128), lambda g: (g, 0, 0)),
            pl.BlockSpec((2, 2, 16, 128), lambda g: (g, 0, 0, 0)),
        ],
        out_specs=pl.BlockSpec((4 * rows, 128), lambda g: (g, 0)),
        compiler_params=pltpu.CompilerParams(vmem_limit_bytes=60 * 2**20),
    )(codes.reshape(8, 2 * HALF, 128), tops)


def solution(mesh):
    in_specs = (P("row", "col"), P(("row", "col"), None), P("row"))
    out_specs = P(None, ("col", "row"))
    return jax.shard_map(shards, mesh=mesh, in_specs=in_specs, out_specs=out_specs, check_vma=False)
```

```python
import functools

import jax
import jax.numpy as jnp
from jax import lax
from jax.experimental import pallas as pl
from jax.experimental.pallas import tpu as pltpu
from jax.sharding import PartitionSpec as P

MESH = pl.DeviceIdType.MESH
SIZES = (160, 160, 128, 128, 64)
TILES = len(SIZES)
STARTS = tuple(sum(SIZES[:t]) for t in range(TILES))
HALF = sum(SIZES)
LIFT = 2.0**40
TOP = 32767.0
STEPS = (
    (1, 0), (3, 0), (0, 1), (0, 3), (1, 1), (3, 3), (1, 3), (3, 1),
    (2, 0), (0, 2), (2, 1), (2, 3), (1, 2), (3, 2), (2, 2),
)


def device(x, y, z, k):
    return (z * 2 + (y >> 1), x * 4 + (y & 1) * 2 + k)


def wait(ref, sem):
    pltpu.make_async_copy(ref, ref, sem).wait()


def ladder_kernel(
    a_ref, i_ref, slot_ref, q_ref, m_ref,
    apad, lhs, onehot, slots, ipack, amp, ints, codes, tops,
    slot_send, slot_recv, half_send, half_recv,
    plane_send, plane_recv, line_send, line_recv, pair_send, pair_recv,
    amp_send, amp_recv, out_send, out_recv, top_send, top_recv,
):
    row, col = lax.axis_index("row"), lax.axis_index("col")
    x, y, z, k = col >> 2, (row & 1) * 2 + ((col >> 1) & 1), row >> 1, col & 1
    yhi_here = row & 1
    xs, ys = [(x + d) & 3 for d in range(4)], [(y + d) & 3 for d in range(4)]
    me = yhi_here * 8 + (col >> 1)

    def chip_of(p):
        return (p & 7) >> 1, (p >> 3) * 2 + (p & 1)

    def place(px, py):
        return (py >> 1) * 8 + px * 2 + (py & 1)

    barrier = pltpu.get_barrier_semaphore()

    def greet(d):
        pl.semaphore_signal(barrier, inc=1, device_id=d, device_id_type=MESH)

    for dx, dy in reversed(STEPS):
        greet(device(xs[dx], ys[dy], z, k))
    for d in range(1, 4):
        for c in range(2):
            greet(device(x, y, (z + d) & 3, c))
    greet(device(x, y, z, 1 - k))
    turned = (y & 1) * 2 + (y >> 1)
    for d in range(1, 4):
        greet(device(x, turned, (z + d) & 3, k))

    def pack(p, _):
        px, py = chip_of(p)
        base = (px * 2 + (py & 1)) * 16 + (py >> 1)
        for zz in range(4):
            for c in range(2):
                at = pl.multiple_of((base + c * 8 + zz * 2) * 128, 128)
                ipack[p, :, (zz * 2 + c) * 128 : (zz * 2 + c + 1) * 128] = i_ref[:, pl.ds(at, 128)]
        return _

    lax.fori_loop(0, 16, pack, None)
    rows = a_ref.shape[0]
    low = rows // 16 * 16
    apad[low:, :] = jnp.zeros((2 * HALF - low, 256), jnp.bfloat16)
    apad[0:rows, :] = a_ref[...]

    def ints_row(zs, p):
        return pl.multiple_of(((zs * 2 + (p >> 3)) * 2 + k) * 256 + (p & 7) * 32, 32)

    mine = pl.ds(ints_row(z, me), 32)
    ints[mine, :] = ipack[me]

    pl.semaphore_wait(barrier, 25)

    def slot_copy(d):
        return pltpu.make_async_remote_copy(
            slot_ref, slots, slot_send.at[d], slot_recv, device_id=device(x, turned, (z + d) & 3, k), device_id_type=MESH
        )

    holds, fixed = z == x, turned == y

    @pl.when(holds)
    def _():
        for d in range(1, 4):
            slot_copy(d).start()

    @pl.when(holds & jnp.logical_not(fixed))
    def _():
        slot_copy(0).start()

    half_copy = pltpu.make_async_remote_copy(
        apad.at[pl.ds(pl.multiple_of((1 - k) * HALF, 32), HALF)],
        lhs.at[:, pl.ds(pl.multiple_of(k * 256, 256), 256)],
        half_send, half_recv, device_id=device(x, y, z, 1 - k), device_id_type=MESH,
    )
    half_copy.start()

    def line_copy(zs, p, to):
        part = ints.at[pl.ds(ints_row(zs, p), 32)]
        pltpu.make_async_remote_copy(
            part, part, line_send, line_recv.at[zs * 16 + p], device_id=device(x, y, to, k), device_id_type=MESH
        ).start()

    def line_wait(zs, p):
        wait(ints.at[pl.ds(ints_row(zs, p), 32)], line_recv.at[zs * 16 + p])

    up, down, far = (z + 1) & 3, (z + 3) & 3, (z + 2) & 3

    def plane_out(steps):
        for dx, dy in steps:
            px, py = xs[dx], ys[dy]
            pltpu.make_async_remote_copy(
                ipack.at[place(px, py)], ints.at[mine], plane_send, plane_recv.at[me],
                device_id=device(px, py, z, k), device_id_type=MESH,
            ).start()

    plane_out(STEPS[:8])
    line_copy(z, me, up)
    line_copy(z, me, down)

    def amp_rows(t, yhi):
        return pl.ds(pl.multiple_of(STARTS[t] * 2 + yhi * SIZES[t], 32), SIZES[t])

    def piece(t, px, py, c):
        return amp.at[
            amp_rows(t, py >> 1),
            pl.ds(pl.multiple_of(px * 1024 + (py & 1) * 512 + c * 256, 256), 256),
        ]

    def at(u, v, c):
        fx, fy = (u, v) if c == 0 else (v, u)
        return xs[fx], ys[fy]

    def amp_sem(t, px, py, c):
        return amp_recv.at[(t * 16 + place(px, py)) * 2 + c]

    def send(t, src, c, to):
        part = piece(t, *src, c)
        pltpu.make_async_remote_copy(
            part, part, amp_send.at[t], amp_sem(t, *src, c), device_id=device(*to, z, k), device_id_type=MESH
        ).start()

    def arrive(t, src, c):
        wait(piece(t, *src, c), amp_sem(t, *src, c))

    def order(t):
        rows = slice(STARTS[t], STARTS[t] + SIZES[t])
        part = jnp.dot(lhs[rows, :], onehot[...], preferred_element_type=jnp.float32)
        amp[amp_rows(t, yhi_here), pl.ds(pl.multiple_of(block * 512, 512), 512)] = part.astype(jnp.bfloat16)

    def first(t):
        for c in range(2):
            for s in (1, 3):
                send(t, at(0, 0, c), c, at(s, 0, c))

    def spread(t, src, c):
        for s in (1, 3):
            send(t, src, c, at(0, s, c))

    def second(t):
        for c in range(2):
            spread(t, at(0, 0, c), c)
            for s in (1, 3):
                arrive(t, at(s, 0, c), c)
                spread(t, at(s, 0, c), c)
            go = 1 + 2 * ((t + c) % 2)
            send(t, at(4 - go, 0, c), c, at(go, 0, c))

    def third(t):
        for c in range(2):
            arrive(t, at(2, 0, c), c)
            spread(t, at(2, 0, c), c)

    def fourth(t):
        for u in (0, 1, 3, 2):
            for c in range(2):
                go = 1 if u % 2 == 0 else 3
                arrive(t, at(u, 4 - go, c), c)
                send(t, at(u, 4 - go, c), c, at(0, go, c))

    def fifth(t):
        for u in range(4):
            for c in range(2):
                go = 1 if u % 2 == 0 else 3
                arrive(t, at(u, go, c), c)
                arrive(t, at(u, 2, c), c)

    def pair_part(zs, yhi, core):
        return ints.at[pl.ds(pl.multiple_of(((zs * 2 + yhi) * 2 + core) * 256, 256), 256)]

    def pair_out(zs):
        for yhi in range(2):
            pltpu.make_async_remote_copy(
                pair_part(zs, yhi, k), pair_part(zs, yhi, k), pair_send, pair_recv.at[zs * 2 + yhi],
                device_id=device(x, y, z, 1 - k), device_id_type=MESH,
            ).start()

    def pair_in(zs):
        for yhi in range(2):
            wait(pair_part(zs, yhi, 1 - k), pair_recv.at[zs * 2 + yhi])

    sources = [me] + [place(xs[-dx % 4], ys[-dy % 4]) for dx, dy in STEPS]

    def plane_in(parts):
        for p in parts:
            wait(ints.at[pl.ds(ints_row(z, p), 32)], plane_recv.at[p])
            line_copy(z, p, up)
            line_copy(z, p, down)

    lhs[:, pl.ds(pl.multiple_of(k * 256, 256), 256)] = apad[pl.ds(pl.multiple_of(k * HALF, 32), HALF), :]

    @pl.when(holds & fixed)
    def _():
        slots[...] = slot_ref[...]

    @pl.when(jnp.logical_not(holds & fixed))
    def _():
        wait(slots, slot_recv)

    block = col >> 1
    for q in range(4):
        want = jnp.broadcast_to(slots[q : q + 1, :] - block * 512, (128, 128)).T
        for s in range(4):
            place_of = lax.broadcasted_iota(jnp.int32, (128, 128), 1) + s * 128
            stored = ((place_of & 255) >> 5) * 64 + (place_of >> 8) * 32 + (place_of & 31)
            hit = jnp.where(want == stored, 1.0, 0.0).astype(jnp.bfloat16)
            onehot[q * 128 : (q + 1) * 128, s * 128 : (s + 1) * 128] = hit
    half_copy.wait()
    order(0)
    first(0)
    plane_out(STEPS[8:])
    order(1)
    first(1)
    plane_in(sources[1:8])
    for t in range(2, TILES):
        order(t)
    plane_in(sources[8:12])
    second(0)
    plane_in(sources[12:])
    pair_out(z)
    third(0)

    def relay(p):
        src, to = (z + 3 + 2 * (p & 1)) & 3, (z + 1 + 2 * (p & 1)) & 3
        line_wait(src, p)
        line_copy(src, p, to)

    def relays(parts):
        for p in parts:
            relay(p)

    relays(sources[0:4])
    first(2)
    second(1)
    fourth(0)
    third(1)
    relays(sources[4:10])
    first(3)
    second(2)
    relays(sources[10:])
    fourth(1)
    third(2)

    def rest(p, _):
        line_wait((z + 1 + 2 * (p & 1)) & 3, p)
        return _

    lax.fori_loop(0, 16, rest, None)
    pair_out(up)
    pair_out(down)
    first(4)
    second(3)

    def last(p, _):
        line_wait(far, p)
        return _

    lax.fori_loop(0, 16, last, None)
    pair_out(far)
    for zs in range(4):
        pair_in(zs)

    def multiply(t):
        size, start = SIZES[t], STARTS[t]

        def one(n, _):
            to = (z + 2 + 3 * n) & 3
            total = jnp.dot(
                amp[2 * start : 2 * (start + size), :],
                ints[:, pl.ds(pl.multiple_of(to * 256, 256), 256)],
                preferred_element_type=jnp.float32,
            )
            for c in range(2):
                for yhi in range(2):
                    part = total[yhi * size : (yhi + 1) * size, c * 128 : (c + 1) * 128]
                    top = jnp.max(jnp.abs(part), axis=0, keepdims=True)
                    scale = TOP / jnp.maximum(top * LIFT, 1e-28)
                    code = jnp.round((part * LIFT) * scale)
                    codes[to * 2 + c, yhi, start : start + size, :] = code.astype(jnp.int32).astype(jnp.int16)
                    tops[to * 2 + c, yhi * 8 + t : yhi * 8 + t + 1, :] = top
                src = codes.at[to * 2 + c, :, pl.ds(start, size)]
                dst = q_ref.at[z, :, pl.ds(pl.multiple_of(k * HALF + start, 32), size)]
                here = (to == z) & (k == c)

                @pl.when(here)
                def _():
                    pltpu.make_async_copy(src, dst, out_recv.at[z * 2 + k]).start()

                @pl.when(jnp.logical_not(here))
                def _():
                    pltpu.make_async_remote_copy(
                        src, dst, out_send.at[t], out_recv.at[z * 2 + k],
                        device_id=device(x, y, to, c), device_id_type=MESH,
                    ).start()

            return _

        lax.fori_loop(0, 4, one, None)

    tops[...] = jnp.zeros_like(tops)

    for t in range(TILES):
        fifth(t)
        multiply(t)
        if t + 4 < TILES and t > 0:
            first(t + 4)
        if t + 3 < TILES and t > 0:
            second(t + 3)
        if t + 2 < TILES:
            fourth(t + 2)
        if t + 3 < TILES:
            third(t + 3)

    for d in range(4):
        for c in range(2):
            to = (z + d) & 3
            src, dst = tops.at[to * 2 + c], m_ref.at[z, k]
            if d:
                pltpu.make_async_remote_copy(
                    src, dst, top_send.at[d * 2 + c], top_recv.at[z * 2 + k],
                    device_id=device(x, y, to, c), device_id_type=MESH,
                ).start()
    other = pltpu.make_async_remote_copy(
        tops.at[z * 2 + 1 - k], m_ref.at[z, k], top_send.at[0], top_recv.at[z * 2 + k],
        device_id=device(x, y, z, 1 - k), device_id_type=MESH,
    )
    other.start()
    pltpu.make_async_copy(tops.at[z * 2 + k], m_ref.at[z, k], top_recv.at[z * 2 + k]).start()

    wait(ipack.at[0:15], plane_send)
    wait(ints.at[0 : 48 * 32], line_send)
    wait(ints.at[0 : 8 * 256], pair_send)
    for t in range(TILES):
        wait(ints.at[0 : 30 * SIZES[t] // 4], amp_send.at[t])
        wait(codes.at[0:7, :, pl.ds(STARTS[t], SIZES[t])], out_send.at[t])

    @pl.when(holds)
    def _():
        for d in range(1, 4):
            slot_copy(d).wait_send()

    @pl.when(holds & jnp.logical_not(fixed))
    def _():
        slot_copy(0).wait_send()

    wait(tops.at[0], top_send.at[0])
    for d in range(1, 4):
        for c in range(2):
            wait(tops.at[0], top_send.at[d * 2 + c])
    for zs in range(4):
        for c in range(2):
            wait(q_ref.at[zs, :, c * HALF : (c + 1) * HALF], out_recv.at[zs * 2 + c])
            wait(m_ref.at[zs, c], top_recv.at[zs * 2 + c])


def decode_kernel(block_rows, q_ref, m_ref, o_ref, codes, values, in_sem, out_sem):
    ins = [pltpu.make_async_copy(q_ref.at[r], codes.at[r], in_sem.at[r]) for r in range(8)]
    for copy in ins:
        copy.start()
    outs = []
    for r in range(8):
        ins[r].wait()
        for h in range(2):
            for t in range(TILES):
                at = h * HALF + STARTS[t]
                rows = min(SIZES[t], block_rows - at)
                if rows <= 0:
                    continue
                code = codes[r, at : at + SIZES[t], :].astype(jnp.int32).astype(jnp.float32)
                line = (r % 2) * 8 + t
                value = (code * (1.0 / TOP)) * m_ref[r // 2, h, line : line + 1, :]
                values[r * block_rows + at : r * block_rows + at + rows, :] = value[0:rows]
        low, high = r * block_rows // 8 * 8, (r + 1) * block_rows // 8 * 8
        copy = pltpu.make_async_copy(values.at[low:high], o_ref.at[low:high], out_sem.at[r])
        copy.start()
        outs.append(copy)
    for copy in outs:
        copy.wait()


def shards(amplitudes, integrals, storage_slot):
    dma = pltpu.SemaphoreType.DMA
    bf16 = jnp.bfloat16
    vmem = pl.BlockSpec(memory_space=pltpu.VMEM)
    hbm = pl.BlockSpec(memory_space=pl.ANY)
    codes, tops = pl.pallas_call(
        ladder_kernel,
        out_shape=(
            jax.ShapeDtypeStruct((4, 2, 2 * HALF, 128), jnp.int16),
            jax.ShapeDtypeStruct((4, 2, 16, 128), jnp.float32),
        ),
        in_specs=[vmem] * 3,
        out_specs=(hbm, hbm),
        scratch_shapes=[
            pltpu.VMEM((2 * HALF, 256), bf16),
            pltpu.VMEM((HALF, 512), bf16),
            pltpu.VMEM((512, 512), bf16),
            pltpu.VMEM((4, 128), jnp.int32),
            pltpu.VMEM((16, 32, 1024), bf16),
            pltpu.VMEM((2 * HALF, 4096), bf16),
            pltpu.VMEM((4096, 1024), bf16),
            pltpu.VMEM((8, 2, HALF, 128), jnp.int16),
            pltpu.VMEM((8, 16, 128), jnp.float32),
            dma((4,)), dma, dma, dma,
            dma, dma((16,)), dma, dma((64,)), dma, dma((8,)),
            dma((TILES,)), dma((TILES * 32,)), dma((TILES,)), dma((8,)), dma((8,)), dma((8,)),
        ],
        compiler_params=pltpu.CompilerParams(
            collective_id=0, has_side_effects=True, vmem_limit_bytes=56 * 2**20
        ),
    )(amplitudes, integrals, storage_slot.reshape(4, 128))
    rows = amplitudes.shape[0]
    return pl.pallas_call(
        functools.partial(decode_kernel, rows),
        out_shape=jax.ShapeDtypeStruct((8 * rows, 128), jnp.float32),
        in_specs=[hbm, vmem],
        out_specs=hbm,
        scratch_shapes=[
            pltpu.VMEM((8, 2 * HALF, 128), jnp.int16),
            pltpu.VMEM((8 * rows, 128), jnp.float32),
            dma((8,)), dma((8,)),
        ],
        compiler_params=pltpu.CompilerParams(vmem_limit_bytes=60 * 2**20),
    )(codes.reshape(8, 2 * HALF, 128), tops)


def solution(mesh):
    in_specs = (P("row", "col"), P(("row", "col"), None), P("row"))
    out_specs = P(None, ("col", "row"))
    return jax.shard_map(shards, mesh=mesh, in_specs=in_specs, out_specs=out_specs, check_vma=False)
```

```python
import functools

import jax
import jax.numpy as jnp
from jax import lax
from jax.experimental import pallas as pl
from jax.experimental.pallas import tpu as pltpu
from jax.sharding import PartitionSpec as P

MESH = pl.DeviceIdType.MESH
SIZES = (160, 128, 128, 128, 96)
TILES = len(SIZES)
STARTS = tuple(sum(SIZES[:t]) for t in range(TILES))
HALF = sum(SIZES)
LIFT = 2.0**40
TOP = 32767.0
STEPS = (
    (1, 0), (3, 0), (0, 1), (0, 3), (1, 1), (3, 3), (1, 3), (3, 1),
    (2, 0), (0, 2), (2, 1), (2, 3), (1, 2), (3, 2), (2, 2),
)


def device(x, y, z, k):
    return (z * 2 + (y >> 1), x * 4 + (y & 1) * 2 + k)


def wait(ref, sem):
    pltpu.make_async_copy(ref, ref, sem).wait()


def ladder_kernel(
    a_hbm, i_hbm, slot_hbm, q_ref, m_ref,
    a_ref, i_ref, slot_ref, in_sem, apad, lhs, onehot, slots, ipack, amp, ints, codes, tops,
    slot_send, slot_recv, half_send, half_recv,
    plane_send, plane_recv, line_send, line_recv, pair_send, pair_recv,
    amp_send, amp_recv, out_send, out_recv, top_send, top_recv,
):
    row, col = lax.axis_index("row"), lax.axis_index("col")
    x, y, z, k = col >> 2, (row & 1) * 2 + ((col >> 1) & 1), row >> 1, col & 1
    yhi_here = row & 1
    xs, ys = [(x + d) & 3 for d in range(4)], [(y + d) & 3 for d in range(4)]
    me = yhi_here * 8 + (col >> 1)

    def chip_of(p):
        return (p & 7) >> 1, (p >> 3) * 2 + (p & 1)

    def place(px, py):
        return (py >> 1) * 8 + px * 2 + (py & 1)

    loads = [
        pltpu.make_async_copy(src, dst, in_sem.at[i])
        for i, (src, dst) in enumerate(((i_hbm, i_ref), (a_hbm, a_ref), (slot_hbm, slot_ref)))
    ]
    for load in loads:
        load.start()

    barrier = pltpu.get_barrier_semaphore()

    def greet(d):
        pl.semaphore_signal(barrier, inc=1, device_id=d, device_id_type=MESH)

    for dx, dy in reversed(STEPS):
        greet(device(xs[dx], ys[dy], z, k))
    for d in range(1, 4):
        for c in range(2):
            greet(device(x, y, (z + d) & 3, c))
    greet(device(x, y, z, 1 - k))
    turned = (y & 1) * 2 + (y >> 1)
    for d in range(1, 4):
        greet(device(x, turned, (z + d) & 3, k))

    def pack(p, _):
        px, py = chip_of(p)
        base = (px * 2 + (py & 1)) * 16 + (py >> 1)
        for zz in range(4):
            for c in range(2):
                at = pl.multiple_of((base + c * 8 + zz * 2) * 128, 128)
                ipack[p, :, (zz * 2 + c) * 128 : (zz * 2 + c + 1) * 128] = i_ref[:, pl.ds(at, 128)]
        return _

    loads[0].wait()
    lax.fori_loop(0, 16, pack, None)
    rows = a_ref.shape[0]
    low = rows // 16 * 16
    apad[0:16, :] = jnp.zeros((16, 256), jnp.bfloat16)
    apad[low:, :] = jnp.zeros((2 * HALF - low, 256), jnp.bfloat16)
    loads[1].wait()
    for r in range(4):

        @pl.when((row & 3) == r)
        def _():
            lead = rows * r % 8
            apad[lead : lead + rows, :] = a_ref[...]

    loads[2].wait()

    def ints_row(zs, p):
        return pl.multiple_of(((zs * 2 + (p >> 3)) * 2 + k) * 256 + (p & 7) * 32, 32)

    mine = pl.ds(ints_row(z, me), 32)
    ints[mine, :] = ipack[me]

    pl.semaphore_wait(barrier, 25)

    def slot_copy(d):
        return pltpu.make_async_remote_copy(
            slot_ref, slots, slot_send.at[d], slot_recv, device_id=device(x, turned, (z + d) & 3, k), device_id_type=MESH
        )

    holds, fixed = z == x, turned == y

    @pl.when(holds)
    def _():
        for d in range(1, 4):
            slot_copy(d).start()

    @pl.when(holds & jnp.logical_not(fixed))
    def _():
        slot_copy(0).start()

    half_copy = pltpu.make_async_remote_copy(
        apad.at[pl.ds(pl.multiple_of((1 - k) * HALF, 32), HALF)],
        lhs.at[:, pl.ds(pl.multiple_of(k * 256, 256), 256)],
        half_send, half_recv, device_id=device(x, y, z, 1 - k), device_id_type=MESH,
    )
    half_copy.start()

    def line_copy(zs, p, to):
        part = ints.at[pl.ds(ints_row(zs, p), 32)]
        pltpu.make_async_remote_copy(
            part, part, line_send, line_recv.at[zs * 16 + p], device_id=device(x, y, to, k), device_id_type=MESH
        ).start()

    def line_wait(zs, p):
        wait(ints.at[pl.ds(ints_row(zs, p), 32)], line_recv.at[zs * 16 + p])

    up, down, far = (z + 1) & 3, (z + 3) & 3, (z + 2) & 3

    def plane_out(steps):
        for dx, dy in steps:
            px, py = xs[dx], ys[dy]
            pltpu.make_async_remote_copy(
                ipack.at[place(px, py)], ints.at[mine], plane_send, plane_recv.at[me],
                device_id=device(px, py, z, k), device_id_type=MESH,
            ).start()

    plane_out(STEPS[:8])
    line_copy(z, me, up)
    line_copy(z, me, down)

    def amp_rows(t, yhi):
        return pl.ds(pl.multiple_of(STARTS[t] * 2 + yhi * SIZES[t], 32), SIZES[t])

    def piece(t, px, py, c):
        return amp.at[
            amp_rows(t, py >> 1),
            pl.ds(pl.multiple_of(px * 1024 + (py & 1) * 512 + c * 256, 256), 256),
        ]

    def at(u, v, c):
        fx, fy = (u, v) if c == 0 else (v, u)
        return xs[fx], ys[fy]

    def amp_sem(t, px, py, c):
        return amp_recv.at[(t * 16 + place(px, py)) * 2 + c]

    def send(t, src, c, to):
        part = piece(t, *src, c)
        pltpu.make_async_remote_copy(
            part, part, amp_send.at[t], amp_sem(t, *src, c), device_id=device(*to, z, k), device_id_type=MESH
        ).start()

    def arrive(t, src, c):
        wait(piece(t, *src, c), amp_sem(t, *src, c))

    def order(t):
        rows = slice(STARTS[t], STARTS[t] + SIZES[t])
        part = jnp.dot(lhs[rows, :], onehot[...], preferred_element_type=jnp.float32)
        amp[amp_rows(t, yhi_here), pl.ds(pl.multiple_of(block * 512, 512), 512)] = part.astype(jnp.bfloat16)

    def first(t):
        for c in range(2):
            for s in (1, 3):
                send(t, at(0, 0, c), c, at(s, 0, c))

    def spread(t, src, c):
        for s in (1, 3):
            send(t, src, c, at(0, s, c))

    def second(t):
        for c in range(2):
            spread(t, at(0, 0, c), c)
            for s in (1, 3):
                arrive(t, at(s, 0, c), c)
                spread(t, at(s, 0, c), c)
            go = 1 + 2 * ((t + c) % 2)
            send(t, at(4 - go, 0, c), c, at(go, 0, c))

    def third(t):
        for c in range(2):
            arrive(t, at(2, 0, c), c)
            spread(t, at(2, 0, c), c)

    def fourth(t):
        for u in (0, 1, 3, 2):
            for c in range(2):
                go = 1 if u % 2 == 0 else 3
                arrive(t, at(u, 4 - go, c), c)
                send(t, at(u, 4 - go, c), c, at(0, go, c))

    def fifth(t):
        for u in range(4):
            for c in range(2):
                go = 1 if u % 2 == 0 else 3
                arrive(t, at(u, go, c), c)
                arrive(t, at(u, 2, c), c)

    def pair_part(zs, yhi, core):
        return ints.at[pl.ds(pl.multiple_of(((zs * 2 + yhi) * 2 + core) * 256, 256), 256)]

    def pair_out(zs):
        for yhi in range(2):
            pltpu.make_async_remote_copy(
                pair_part(zs, yhi, k), pair_part(zs, yhi, k), pair_send, pair_recv.at[zs * 2 + yhi],
                device_id=device(x, y, z, 1 - k), device_id_type=MESH,
            ).start()

    def pair_in(zs):
        for yhi in range(2):
            wait(pair_part(zs, yhi, 1 - k), pair_recv.at[zs * 2 + yhi])

    sources = [me] + [place(xs[-dx % 4], ys[-dy % 4]) for dx, dy in STEPS]

    def plane_in(parts):
        for p in parts:
            wait(ints.at[pl.ds(ints_row(z, p), 32)], plane_recv.at[p])
            line_copy(z, p, up)
            line_copy(z, p, down)

    lhs[:, pl.ds(pl.multiple_of(k * 256, 256), 256)] = apad[pl.ds(pl.multiple_of(k * HALF, 32), HALF), :]

    @pl.when(holds & fixed)
    def _():
        slots[...] = slot_ref[...]

    @pl.when(jnp.logical_not(holds & fixed))
    def _():
        wait(slots, slot_recv)

    block = col >> 1
    for q in range(4):
        want = jnp.broadcast_to(slots[q : q + 1, :] - block * 512, (128, 128)).T
        for s in range(4):
            place_of = lax.broadcasted_iota(jnp.int32, (128, 128), 1) + s * 128
            stored = ((place_of & 255) >> 5) * 64 + (place_of >> 8) * 32 + (place_of & 31)
            hit = jnp.where(want == stored, 1.0, 0.0).astype(jnp.bfloat16)
            onehot[q * 128 : (q + 1) * 128, s * 128 : (s + 1) * 128] = hit
    half_copy.wait()
    def relay(p):
        src, to = (z + 3 + 2 * (p & 1)) & 3, (z + 1 + 2 * (p & 1)) & 3
        line_wait(src, p)
        line_copy(src, p, to)

    def relays(parts):
        for p in parts:
            relay(p)

    def rest(p, _):
        line_wait((z + 1 + 2 * (p & 1)) & 3, p)
        return _

    def last(p, _):
        line_wait(far, p)
        return _

    def multiply(t):
        size, start = SIZES[t], STARTS[t]

        def one(n, _):
            to = (z + 2 + 3 * n) & 3
            total = jnp.dot(
                amp[2 * start : 2 * (start + size), :],
                ints[:, pl.ds(pl.multiple_of(to * 256, 256), 256)],
                preferred_element_type=jnp.float32,
            )
            for c in range(2):
                for yhi in range(2):
                    part = total[yhi * size : (yhi + 1) * size, c * 128 : (c + 1) * 128]
                    top = jnp.max(jnp.abs(part), axis=0, keepdims=True)
                    scale = TOP / jnp.maximum(top * LIFT, 1e-28)
                    code = jnp.round((part * LIFT) * scale)
                    codes[to * 2 + c, yhi, start : start + size, :] = code.astype(jnp.int32).astype(jnp.int16)
                    tops[to * 2 + c, yhi * 8 + t : yhi * 8 + t + 1, :] = top
                src = codes.at[to * 2 + c, :, pl.ds(start, size)]
                dst = q_ref.at[z, :, pl.ds(pl.multiple_of(k * HALF + start, 32), size)]
                here = (to == z) & (k == c)

                @pl.when(here)
                def _():
                    pltpu.make_async_copy(src, dst, out_recv.at[z * 2 + k]).start()

                @pl.when(jnp.logical_not(here))
                def _():
                    pltpu.make_async_remote_copy(
                        src, dst, out_send.at[t], out_recv.at[z * 2 + k],
                        device_id=device(x, y, to, c), device_id_type=MESH,
                    ).start()

            return _

        lax.fori_loop(0, 4, one, None)

    tops[...] = jnp.zeros_like(tops)

    order(0)
    first(0)
    plane_out(STEPS[8:])
    order(1)
    first(1)
    plane_in(sources[1:8])
    order(2)
    order(3)
    order(4)
    plane_in(sources[8:12])
    second(0)
    plane_in(sources[12:16])
    pair_out(z)
    third(0)
    first(2)
    second(1)
    relays(sources[0:6])
    fourth(0)
    third(1)
    first(3)
    second(2)
    relays(sources[6:16])
    fourth(1)
    third(2)
    lax.fori_loop(0, 16, rest, None)
    pair_out(up)
    pair_out(down)
    first(4)
    second(3)
    lax.fori_loop(0, 16, last, None)
    pair_out(far)
    for zs in range(4):
        pair_in(zs)
    fifth(0)
    multiply(0)
    fourth(2)
    third(3)
    second(4)
    fifth(1)
    multiply(1)
    fourth(3)
    third(4)
    fifth(2)
    multiply(2)
    fourth(4)
    fifth(3)
    multiply(3)
    fifth(4)
    multiply(4)

    for d in range(4):
        for c in range(2):
            to = (z + d) & 3
            src, dst = tops.at[to * 2 + c], m_ref.at[z, k]
            if d:
                pltpu.make_async_remote_copy(
                    src, dst, top_send.at[d * 2 + c], top_recv.at[z * 2 + k],
                    device_id=device(x, y, to, c), device_id_type=MESH,
                ).start()
    other = pltpu.make_async_remote_copy(
        tops.at[z * 2 + 1 - k], m_ref.at[z, k], top_send.at[0], top_recv.at[z * 2 + k],
        device_id=device(x, y, z, 1 - k), device_id_type=MESH,
    )
    other.start()
    pltpu.make_async_copy(tops.at[z * 2 + k], m_ref.at[z, k], top_recv.at[z * 2 + k]).start()

    wait(ipack.at[0:15], plane_send)
    wait(ints.at[0 : 48 * 32], line_send)
    wait(ints.at[0 : 8 * 256], pair_send)
    for t in range(TILES):
        wait(ints.at[0 : 30 * SIZES[t] // 4], amp_send.at[t])
        wait(codes.at[0:7, :, pl.ds(STARTS[t], SIZES[t])], out_send.at[t])

    @pl.when(holds)
    def _():
        for d in range(1, 4):
            slot_copy(d).wait_send()

    @pl.when(holds & jnp.logical_not(fixed))
    def _():
        slot_copy(0).wait_send()

    wait(tops.at[0], top_send.at[0])
    for d in range(1, 4):
        for c in range(2):
            wait(tops.at[0], top_send.at[d * 2 + c])
    for zs in range(4):
        for c in range(2):
            wait(q_ref.at[zs, :, c * HALF : (c + 1) * HALF], out_recv.at[zs * 2 + c])
            wait(m_ref.at[zs, c], top_recv.at[zs * 2 + c])


def decode_kernel(block_rows, q_ref, m_ref, o_ref, codes, values, in_sem, out_sem):
    ins = [pltpu.make_async_copy(q_ref.at[r], codes.at[r], in_sem.at[r]) for r in range(8)]
    for copy in ins:
        copy.start()
    outs = []
    for r in range(8):
        ins[r].wait()
        lead = r * block_rows % 8
        base, end = r * block_rows - lead, lead + block_rows
        for h in range(2):
            for t in range(TILES):
                start = h * HALF + STARTS[t]
                stop = min(start + SIZES[t], end)
                line = (r % 2) * 8 + t
                top = m_ref[r // 2, h, line : line + 1, :]
                cuts = [max(start, lead), stop]
                if lead and start == 0:
                    cuts.insert(1, 8)
                if stop % 8:
                    cuts.insert(-1, stop // 8 * 8)
                for a, b in zip(cuts, cuts[1:]):
                    code = codes[r, a:b, :].astype(jnp.int32).astype(jnp.float32)
                    values[base + a : base + b, :] = (code * (1.0 / TOP)) * top
        low, high = base, (r + 1) * block_rows // 8 * 8
        copy = pltpu.make_async_copy(values.at[low:high], o_ref.at[low:high], out_sem.at[r])
        copy.start()
        outs.append(copy)
    for copy in outs:
        copy.wait()


def shards(amplitudes, integrals, storage_slot):
    dma = pltpu.SemaphoreType.DMA
    bf16 = jnp.bfloat16
    vmem = pl.BlockSpec(memory_space=pltpu.VMEM)
    hbm = pl.BlockSpec(memory_space=pl.ANY)
    codes, tops = pl.pallas_call(
        ladder_kernel,
        out_shape=(
            jax.ShapeDtypeStruct((4, 2, 2 * HALF, 128), jnp.int16),
            jax.ShapeDtypeStruct((4, 2, 16, 128), jnp.float32),
        ),
        in_specs=[hbm] * 3,
        out_specs=(hbm, hbm),
        scratch_shapes=[
            pltpu.VMEM(amplitudes.shape, bf16),
            pltpu.VMEM(integrals.shape, bf16),
            pltpu.VMEM((4, 128), jnp.int32),
            dma((3,)),
            pltpu.VMEM((2 * HALF, 256), bf16),
            pltpu.VMEM((HALF, 512), bf16),
            pltpu.VMEM((512, 512), bf16),
            pltpu.VMEM((4, 128), jnp.int32),
            pltpu.VMEM((16, 32, 1024), bf16),
            pltpu.VMEM((2 * HALF, 4096), bf16),
            pltpu.VMEM((4096, 1024), bf16),
            pltpu.VMEM((8, 2, HALF, 128), jnp.int16),
            pltpu.VMEM((8, 16, 128), jnp.float32),
            dma((4,)), dma, dma, dma,
            dma, dma((16,)), dma, dma((64,)), dma, dma((8,)),
            dma((TILES,)), dma((TILES * 32,)), dma((TILES,)), dma((8,)), dma((8,)), dma((8,)),
        ],
        compiler_params=pltpu.CompilerParams(
            collective_id=0, has_side_effects=True, vmem_limit_bytes=56 * 2**20
        ),
    )(amplitudes, integrals, storage_slot.reshape(4, 128))
    rows = amplitudes.shape[0]
    return pl.pallas_call(
        functools.partial(decode_kernel, rows),
        out_shape=jax.ShapeDtypeStruct((8 * rows, 128), jnp.float32),
        in_specs=[hbm, vmem],
        out_specs=hbm,
        scratch_shapes=[
            pltpu.VMEM((8, 2 * HALF, 128), jnp.int16),
            pltpu.VMEM((8 * rows, 128), jnp.float32),
            dma((8,)), dma((8,)),
        ],
        compiler_params=pltpu.CompilerParams(vmem_limit_bytes=60 * 2**20),
    )(codes.reshape(8, 2 * HALF, 128), tops)


def solution(mesh):
    in_specs = (P("row", "col"), P(("row", "col"), None), P("row"))
    out_specs = P(None, ("col", "row"))
    return jax.shard_map(shards, mesh=mesh, in_specs=in_specs, out_specs=out_specs, check_vma=False)
```

```python
import functools

import jax
import jax.numpy as jnp
from jax import lax
from jax.experimental import pallas as pl
from jax.experimental.pallas import tpu as pltpu
from jax.sharding import PartitionSpec as P

MESH = pl.DeviceIdType.MESH
SIZES = (160, 128, 128, 128, 96)
TILES = len(SIZES)
STARTS = tuple(sum(SIZES[:t]) for t in range(TILES))
HALF = sum(SIZES)
LIFT = 2.0**40
TOP = 32767.0
STEPS = (
    (1, 0), (3, 0), (0, 1), (0, 3), (1, 1), (3, 3), (1, 3), (3, 1),
    (2, 0), (0, 2), (2, 1), (2, 3), (1, 2), (3, 2), (2, 2),
)


def device(x, y, z, k):
    return (z * 2 + (y >> 1), x * 4 + (y & 1) * 2 + k)


def wait(ref, sem):
    pltpu.make_async_copy(ref, ref, sem).wait()


def ladder_kernel(
    a_hbm, i_hbm, slot_hbm, q_ref, m_ref,
    a_ref, i_ref, slot_ref, in_sem, apad, lhs, onehot, slots, ipack, amp, ints, codes, tops,
    slot_send, slot_recv, half_send, half_recv,
    plane_send, plane_recv, line_send, line_recv, pair_send, pair_recv,
    amp_send, amp_recv, out_send, out_recv, top_send, top_recv,
):
    row, col = lax.axis_index("row"), lax.axis_index("col")
    x, y, z, k = col >> 2, (row & 1) * 2 + ((col >> 1) & 1), row >> 1, col & 1
    yhi_here = row & 1
    xs, ys = [(x + d) & 3 for d in range(4)], [(y + d) & 3 for d in range(4)]
    me = yhi_here * 8 + (col >> 1)

    def chip_of(p):
        return (p & 7) >> 1, (p >> 3) * 2 + (p & 1)

    def place(px, py):
        return (py >> 1) * 8 + px * 2 + (py & 1)

    loads = [
        pltpu.make_async_copy(src, dst, in_sem.at[i])
        for i, (src, dst) in enumerate(((i_hbm, i_ref), (a_hbm, a_ref), (slot_hbm, slot_ref)))
    ]
    for load in loads:
        load.start()

    barrier = pltpu.get_barrier_semaphore()

    def greet(d):
        pl.semaphore_signal(barrier, inc=1, device_id=d, device_id_type=MESH)

    for dx, dy in reversed(STEPS):
        greet(device(xs[dx], ys[dy], z, k))
    for d in range(1, 4):
        for c in range(2):
            greet(device(x, y, (z + d) & 3, c))
    greet(device(x, y, z, 1 - k))
    turned = (y & 1) * 2 + (y >> 1)
    for d in range(1, 4):
        greet(device(x, turned, (z + d) & 3, k))

    def pack(p, _):
        px, py = chip_of(p)
        base = (px * 2 + (py & 1)) * 16 + (py >> 1)
        for zz in range(4):
            for c in range(2):
                at = pl.multiple_of((base + c * 8 + zz * 2) * 128, 128)
                ipack[p, :, (zz * 2 + c) * 128 : (zz * 2 + c + 1) * 128] = i_ref[:, pl.ds(at, 128)]
        return _

    loads[0].wait()
    lax.fori_loop(0, 16, pack, None)
    rows = a_ref.shape[0]
    low = rows // 16 * 16
    apad[0:16, :] = jnp.zeros((16, 256), jnp.bfloat16)
    apad[low:, :] = jnp.zeros((2 * HALF - low, 256), jnp.bfloat16)
    loads[1].wait()
    for r in range(4):

        @pl.when((row & 3) == r)
        def _():
            lead = rows * r % 8
            apad[lead : lead + rows, :] = a_ref[...]

    loads[2].wait()

    def ints_row(zs, p):
        return pl.multiple_of(((zs * 2 + (p >> 3)) * 2 + k) * 256 + (p & 7) * 32, 32)

    mine = pl.ds(ints_row(z, me), 32)
    ints[mine, :] = ipack[me]

    pl.semaphore_wait(barrier, 25)

    def slot_copy(d):
        return pltpu.make_async_remote_copy(
            slot_ref, slots, slot_send.at[d], slot_recv, device_id=device(x, turned, (z + d) & 3, k), device_id_type=MESH
        )

    holds, fixed = z == x, turned == y

    @pl.when(holds)
    def _():
        for d in range(1, 4):
            slot_copy(d).start()

    @pl.when(holds & jnp.logical_not(fixed))
    def _():
        slot_copy(0).start()

    half_copy = pltpu.make_async_remote_copy(
        apad.at[pl.ds(pl.multiple_of((1 - k) * HALF, 32), HALF)],
        lhs.at[:, pl.ds(pl.multiple_of(k * 256, 256), 256)],
        half_send, half_recv, device_id=device(x, y, z, 1 - k), device_id_type=MESH,
    )
    half_copy.start()

    def line_copy(zs, p, to):
        part = ints.at[pl.ds(ints_row(zs, p), 32)]
        pltpu.make_async_remote_copy(
            part, part, line_send, line_recv.at[zs * 16 + p], device_id=device(x, y, to, k), device_id_type=MESH
        ).start()

    def line_wait(zs, p):
        wait(ints.at[pl.ds(ints_row(zs, p), 32)], line_recv.at[zs * 16 + p])

    up, down, far = (z + 1) & 3, (z + 3) & 3, (z + 2) & 3

    def plane_out(steps):
        for dx, dy in steps:
            px, py = xs[dx], ys[dy]
            pltpu.make_async_remote_copy(
                ipack.at[place(px, py)], ints.at[mine], plane_send, plane_recv.at[me],
                device_id=device(px, py, z, k), device_id_type=MESH,
            ).start()

    plane_out(STEPS[:8])
    line_copy(z, me, up)
    line_copy(z, me, down)

    def amp_rows(t, yhi):
        return pl.ds(pl.multiple_of(STARTS[t] * 2 + yhi * SIZES[t], 32), SIZES[t])

    def piece(t, px, py, c):
        return amp.at[
            amp_rows(t, py >> 1),
            pl.ds(pl.multiple_of(px * 1024 + (py & 1) * 512 + c * 256, 256), 256),
        ]

    def at(u, v, c):
        fx, fy = (u, v) if c == 0 else (v, u)
        return xs[fx], ys[fy]

    def amp_sem(t, px, py, c):
        return amp_recv.at[(t * 16 + place(px, py)) * 2 + c]

    def send(t, src, c, to):
        part = piece(t, *src, c)
        pltpu.make_async_remote_copy(
            part, part, amp_send.at[t], amp_sem(t, *src, c), device_id=device(*to, z, k), device_id_type=MESH
        ).start()

    def arrive(t, src, c):
        wait(piece(t, *src, c), amp_sem(t, *src, c))

    def order(t):
        rows = slice(STARTS[t], STARTS[t] + SIZES[t])
        part = jnp.dot(lhs[rows, :], onehot[...], preferred_element_type=jnp.float32)
        amp[amp_rows(t, yhi_here), pl.ds(pl.multiple_of(block * 512, 512), 512)] = part.astype(jnp.bfloat16)

    def first(t):
        for c in range(2):
            for s in (1, 3):
                send(t, at(0, 0, c), c, at(s, 0, c))

    def spread(t, src, c):
        for s in (1, 3):
            send(t, src, c, at(0, s, c))

    def second(t):
        for c in range(2):
            spread(t, at(0, 0, c), c)
            for s in (1, 3):
                arrive(t, at(s, 0, c), c)
                spread(t, at(s, 0, c), c)
            go = 1 + 2 * ((t + c) % 2)
            send(t, at(4 - go, 0, c), c, at(go, 0, c))

    def third(t):
        for c in range(2):
            arrive(t, at(2, 0, c), c)
            spread(t, at(2, 0, c), c)

    def fourth(t):
        for u in (0, 1, 3, 2):
            for c in range(2):
                go = 1 if u % 2 == 0 else 3
                arrive(t, at(u, 4 - go, c), c)
                send(t, at(u, 4 - go, c), c, at(0, go, c))

    def fifth(t):
        for u in range(4):
            for c in range(2):
                go = 1 if u % 2 == 0 else 3
                arrive(t, at(u, go, c), c)
                arrive(t, at(u, 2, c), c)

    def pair_part(zs, yhi, core):
        return ints.at[pl.ds(pl.multiple_of(((zs * 2 + yhi) * 2 + core) * 256, 256), 256)]

    def pair_out(zs):
        for yhi in range(2):
            pltpu.make_async_remote_copy(
                pair_part(zs, yhi, k), pair_part(zs, yhi, k), pair_send, pair_recv.at[zs * 2 + yhi],
                device_id=device(x, y, z, 1 - k), device_id_type=MESH,
            ).start()

    def pair_in(zs):
        for yhi in range(2):
            wait(pair_part(zs, yhi, 1 - k), pair_recv.at[zs * 2 + yhi])

    sources = [me] + [place(xs[-dx % 4], ys[-dy % 4]) for dx, dy in STEPS]

    def plane_in(parts):
        for p in parts:
            wait(ints.at[pl.ds(ints_row(z, p), 32)], plane_recv.at[p])
            line_copy(z, p, up)
            line_copy(z, p, down)

    lhs[:, pl.ds(pl.multiple_of(k * 256, 256), 256)] = apad[pl.ds(pl.multiple_of(k * HALF, 32), HALF), :]

    @pl.when(holds & fixed)
    def _():
        slots[...] = slot_ref[...]

    @pl.when(jnp.logical_not(holds & fixed))
    def _():
        wait(slots, slot_recv)

    block = col >> 1
    for q in range(4):
        want = jnp.broadcast_to(slots[q : q + 1, :] - block * 512, (128, 128)).T
        for s in range(4):
            place_of = lax.broadcasted_iota(jnp.int32, (128, 128), 1) + s * 128
            stored = ((place_of & 255) >> 5) * 64 + (place_of >> 8) * 32 + (place_of & 31)
            hit = jnp.where(want == stored, 1.0, 0.0).astype(jnp.bfloat16)
            onehot[q * 128 : (q + 1) * 128, s * 128 : (s + 1) * 128] = hit
    half_copy.wait()
    def relay(p):
        src, to = (z + 3 + 2 * (p & 1)) & 3, (z + 1 + 2 * (p & 1)) & 3
        line_wait(src, p)
        line_copy(src, p, to)

    def relays(parts):
        for p in parts:
            relay(p)

    def rest(p, _):
        line_wait((z + 1 + 2 * (p & 1)) & 3, p)
        return _

    def last(p, _):
        line_wait(far, p)
        return _

    def multiply(t):
        size, start = SIZES[t], STARTS[t]

        def one(n, _):
            to = (z + 2 + 3 * n) & 3
            total = jnp.dot(
                amp[2 * start : 2 * (start + size), :],
                ints[:, pl.ds(pl.multiple_of(to * 256, 256), 256)],
                preferred_element_type=jnp.float32,
            )
            for c in range(2):
                for yhi in range(2):
                    part = total[yhi * size : (yhi + 1) * size, c * 128 : (c + 1) * 128]
                    top = jnp.max(jnp.abs(part), axis=0, keepdims=True)
                    scale = TOP / jnp.maximum(top * LIFT, 1e-28)
                    code = jnp.round((part * LIFT) * scale)
                    codes[to * 2 + c, yhi, start : start + size, :] = code.astype(jnp.int32).astype(jnp.int16)
                    tops[to * 2 + c, yhi * 8 + t : yhi * 8 + t + 1, :] = top
                src = codes.at[to * 2 + c, :, pl.ds(start, size)]
                dst = q_ref.at[z, :, pl.ds(pl.multiple_of(k * HALF + start, 32), size)]
                here = (to == z) & (k == c)

                @pl.when(here)
                def _():
                    pltpu.make_async_copy(src, dst, out_recv.at[z * 2 + k]).start()

                @pl.when(jnp.logical_not(here))
                def _():
                    pltpu.make_async_remote_copy(
                        src, dst, out_send.at[t], out_recv.at[z * 2 + k],
                        device_id=device(x, y, to, c), device_id_type=MESH,
                    ).start()

            return _

        lax.fori_loop(0, 4, one, None)

    tops[...] = jnp.zeros_like(tops)

    order(0)
    first(0)
    plane_out(STEPS[8:])
    order(1)
    first(1)
    plane_in(sources[1:8])
    order(2)
    order(3)
    order(4)
    plane_in(sources[8:12])
    second(0)
    plane_in(sources[12:16])
    pair_out(z)
    third(0)
    first(2)
    second(1)
    relays(sources[0:6])
    fourth(0)
    third(1)
    first(3)
    second(2)
    relays(sources[6:16])
    fourth(1)
    third(2)
    lax.fori_loop(0, 16, rest, None)
    pair_out(up)
    pair_out(down)
    first(4)
    second(3)
    lax.fori_loop(0, 16, last, None)
    pair_out(far)
    for zs in range(4):
        pair_in(zs)
    fifth(0)
    multiply(0)
    fourth(2)
    third(3)
    second(4)
    fifth(1)
    multiply(1)
    fourth(3)
    third(4)
    fifth(2)
    multiply(2)
    fourth(4)
    fifth(3)
    multiply(3)
    fifth(4)
    multiply(4)

    for d in range(4):
        for c in range(2):
            to = (z + d) & 3
            src, dst = tops.at[to * 2 + c], m_ref.at[z, k]
            if d:
                pltpu.make_async_remote_copy(
                    src, dst, top_send.at[d * 2 + c], top_recv.at[z * 2 + k],
                    device_id=device(x, y, to, c), device_id_type=MESH,
                ).start()
    other = pltpu.make_async_remote_copy(
        tops.at[z * 2 + 1 - k], m_ref.at[z, k], top_send.at[0], top_recv.at[z * 2 + k],
        device_id=device(x, y, z, 1 - k), device_id_type=MESH,
    )
    other.start()
    pltpu.make_async_copy(tops.at[z * 2 + k], m_ref.at[z, k], top_recv.at[z * 2 + k]).start()

    wait(ipack.at[0:15], plane_send)
    wait(ints.at[0 : 48 * 32], line_send)
    wait(ints.at[0 : 8 * 256], pair_send)
    for t in range(TILES):
        wait(ints.at[0 : 30 * SIZES[t] // 4], amp_send.at[t])
        wait(codes.at[0:7, :, pl.ds(STARTS[t], SIZES[t])], out_send.at[t])

    @pl.when(holds)
    def _():
        for d in range(1, 4):
            slot_copy(d).wait_send()

    @pl.when(holds & jnp.logical_not(fixed))
    def _():
        slot_copy(0).wait_send()

    wait(tops.at[0], top_send.at[0])
    for d in range(1, 4):
        for c in range(2):
            wait(tops.at[0], top_send.at[d * 2 + c])
    for zs in range(4):
        for c in range(2):
            wait(q_ref.at[zs, :, c * HALF : (c + 1) * HALF], out_recv.at[zs * 2 + c])
            wait(m_ref.at[zs, c], top_recv.at[zs * 2 + c])


def decode_kernel(block_rows, q_ref, m_ref, o_ref, values, out_sem):
    outs = []
    for r in range(8):
        lead = r * block_rows % 8
        base, end = r * block_rows - lead, lead + block_rows
        for h in range(2):
            for t in range(TILES):
                start = h * HALF + STARTS[t]
                stop = min(start + SIZES[t], end)
                line = (r % 2) * 8 + t
                top = m_ref[r // 2, h, line : line + 1, :]
                cuts = [max(start, lead), stop]
                if lead and start == 0:
                    cuts.insert(1, 8)
                if stop % 8:
                    cuts.insert(-1, stop // 8 * 8)
                for a, b in zip(cuts, cuts[1:]):
                    code = q_ref[r, a:b, :].astype(jnp.int32).astype(jnp.float32)
                    values[base + a : base + b, :] = (code * (1.0 / TOP)) * top
        low, high = base, (r + 1) * block_rows // 8 * 8
        copy = pltpu.make_async_copy(values.at[low:high], o_ref.at[low:high], out_sem.at[r])
        copy.start()
        outs.append(copy)
    for copy in outs:
        copy.wait()


def shards(amplitudes, integrals, storage_slot):
    dma = pltpu.SemaphoreType.DMA
    bf16 = jnp.bfloat16
    vmem = pl.BlockSpec(memory_space=pltpu.VMEM)
    hbm = pl.BlockSpec(memory_space=pl.ANY)
    codes, tops = pl.pallas_call(
        ladder_kernel,
        out_shape=(
            pltpu.VMEM((4, 2, 2 * HALF, 128), jnp.int16),
            pltpu.VMEM((4, 2, 16, 128), jnp.float32),
        ),
        in_specs=[hbm] * 3,
        out_specs=(vmem, vmem),
        scratch_shapes=[
            pltpu.VMEM(amplitudes.shape, bf16),
            pltpu.VMEM(integrals.shape, bf16),
            pltpu.VMEM((4, 128), jnp.int32),
            dma((3,)),
            pltpu.VMEM((2 * HALF, 256), bf16),
            pltpu.VMEM((HALF, 512), bf16),
            pltpu.VMEM((512, 512), bf16),
            pltpu.VMEM((4, 128), jnp.int32),
            pltpu.VMEM((16, 32, 1024), bf16),
            pltpu.VMEM((2 * HALF, 4096), bf16),
            pltpu.VMEM((4096, 1024), bf16),
            pltpu.VMEM((8, 2, HALF, 128), jnp.int16),
            pltpu.VMEM((8, 16, 128), jnp.float32),
            dma((4,)), dma, dma, dma,
            dma, dma((16,)), dma, dma((64,)), dma, dma((8,)),
            dma((TILES,)), dma((TILES * 32,)), dma((TILES,)), dma((8,)), dma((8,)), dma((8,)),
        ],
        compiler_params=pltpu.CompilerParams(
            collective_id=0, has_side_effects=True, vmem_limit_bytes=57 * 2**20
        ),
    )(amplitudes, integrals, storage_slot.reshape(4, 128))
    rows = amplitudes.shape[0]
    return pl.pallas_call(
        functools.partial(decode_kernel, rows),
        out_shape=jax.ShapeDtypeStruct((8 * rows, 128), jnp.float32),
        in_specs=[vmem, vmem],
        out_specs=hbm,
        scratch_shapes=[
            pltpu.VMEM((8 * rows, 128), jnp.float32),
            dma((8,)),
        ],
        compiler_params=pltpu.CompilerParams(vmem_limit_bytes=32 * 2**20),
    )(codes.reshape(8, 2 * HALF, 128), tops)


def solution(mesh):
    in_specs = (P("row", "col"), P(("row", "col"), None), P("row"))
    out_specs = P(None, ("col", "row"))
    return jax.shard_map(shards, mesh=mesh, in_specs=in_specs, out_specs=out_specs, check_vma=False)
```

```python
import functools

import jax
import jax.numpy as jnp
from jax import lax
from jax.experimental import pallas as pl
from jax.experimental.pallas import tpu as pltpu
from jax.sharding import PartitionSpec as P

MESH = pl.DeviceIdType.MESH
SIZES = (160, 128, 128, 128, 96)
TILES = len(SIZES)
STARTS = tuple(sum(SIZES[:t]) for t in range(TILES))
HALF = sum(SIZES)
LIFT = 2.0**40
TOP = 32767.0
STEPS = (
    (1, 0), (3, 0), (0, 1), (0, 3), (1, 1), (3, 3), (1, 3), (3, 1),
    (2, 0), (0, 2), (2, 1), (2, 3), (1, 2), (3, 2), (2, 2),
)


def device(x, y, z, k):
    return (z * 2 + (y >> 1), x * 4 + (y & 1) * 2 + k)


def wait(ref, sem):
    pltpu.make_async_copy(ref, ref, sem).wait()


def ladder_kernel(
    a_hbm, i_hbm, slot_hbm, q_ref, m_ref,
    a_ref, i_ref, slot_ref, in_sem, apad, lhs, onehot, slots, ipack, amp, ints, codes, tops,
    slot_send, slot_recv, half_send, half_recv,
    plane_send, plane_recv, line_send, line_recv, pair_send, pair_recv,
    amp_send, amp_recv, out_send, out_recv, top_send, top_recv,
):
    row, col = lax.axis_index("row"), lax.axis_index("col")
    x, y, z, k = col >> 2, (row & 1) * 2 + ((col >> 1) & 1), row >> 1, col & 1
    yhi_here = row & 1
    xs, ys = [(x + d) & 3 for d in range(4)], [(y + d) & 3 for d in range(4)]
    me = yhi_here * 8 + (col >> 1)

    def chip_of(p):
        return (p & 7) >> 1, (p >> 3) * 2 + (p & 1)

    def place(px, py):
        return (py >> 1) * 8 + px * 2 + (py & 1)

    loads = [
        pltpu.make_async_copy(src, dst, in_sem.at[i])
        for i, (src, dst) in enumerate(((i_hbm, i_ref), (a_hbm, a_ref), (slot_hbm, slot_ref)))
    ]
    for load in loads:
        load.start()

    barrier = pltpu.get_barrier_semaphore()

    def greet(d):
        pl.semaphore_signal(barrier, inc=1, device_id=d, device_id_type=MESH)

    for dx, dy in reversed(STEPS):
        greet(device(xs[dx], ys[dy], z, k))
    for d in range(1, 4):
        for c in range(2):
            greet(device(x, y, (z + d) & 3, c))
    greet(device(x, y, z, 1 - k))
    turned = (y & 1) * 2 + (y >> 1)
    for d in range(1, 4):
        greet(device(x, turned, (z + d) & 3, k))

    def pack(p, _):
        px, py = chip_of(p)
        base = (px * 2 + (py & 1)) * 16 + (py >> 1)
        for zz in range(4):
            for c in range(2):
                at = pl.multiple_of((base + c * 8 + zz * 2) * 128, 128)
                ipack[p, :, (zz * 2 + c) * 128 : (zz * 2 + c + 1) * 128] = i_ref[:, pl.ds(at, 128)]
        return _

    loads[0].wait()
    lax.fori_loop(0, 16, pack, None)
    rows = a_ref.shape[0]
    low = rows // 16 * 16
    apad[0:16, :] = jnp.zeros((16, 256), jnp.bfloat16)
    apad[low:, :] = jnp.zeros((2 * HALF - low, 256), jnp.bfloat16)
    loads[1].wait()
    for r in range(4):

        @pl.when((row & 3) == r)
        def _():
            lead = rows * r % 8
            apad[lead : lead + rows, :] = a_ref[...]

    loads[2].wait()

    def ints_row(zs, p):
        return pl.multiple_of(((zs * 2 + (p >> 3)) * 2 + k) * 256 + (p & 7) * 32, 32)

    mine = pl.ds(ints_row(z, me), 32)
    ints[mine, :] = ipack[me]

    pl.semaphore_wait(barrier, 25)

    def slot_copy(d):
        return pltpu.make_async_remote_copy(
            slot_ref, slots, slot_send.at[d], slot_recv, device_id=device(x, turned, (z + d) & 3, k), device_id_type=MESH
        )

    holds, fixed = z == x, turned == y

    @pl.when(holds)
    def _():
        for d in range(1, 4):
            slot_copy(d).start()

    @pl.when(holds & jnp.logical_not(fixed))
    def _():
        slot_copy(0).start()

    half_copy = pltpu.make_async_remote_copy(
        apad.at[pl.ds(pl.multiple_of((1 - k) * HALF, 32), HALF)],
        lhs.at[:, pl.ds(pl.multiple_of(k * 256, 256), 256)],
        half_send, half_recv, device_id=device(x, y, z, 1 - k), device_id_type=MESH,
    )
    half_copy.start()

    def line_copy(zs, p, to):
        part = ints.at[pl.ds(ints_row(zs, p), 32)]
        pltpu.make_async_remote_copy(
            part, part, line_send, line_recv.at[zs * 16 + p], device_id=device(x, y, to, k), device_id_type=MESH
        ).start()

    def line_wait(zs, p):
        wait(ints.at[pl.ds(ints_row(zs, p), 32)], line_recv.at[zs * 16 + p])

    up, down, far = (z + 1) & 3, (z + 3) & 3, (z + 2) & 3

    def plane_out(steps):
        for dx, dy in steps:
            px, py = xs[dx], ys[dy]
            pltpu.make_async_remote_copy(
                ipack.at[place(px, py)], ints.at[mine], plane_send, plane_recv.at[me],
                device_id=device(px, py, z, k), device_id_type=MESH,
            ).start()

    plane_out(STEPS[:8])
    line_copy(z, me, up)
    line_copy(z, me, down)

    def amp_rows(t, yhi):
        return pl.ds(pl.multiple_of(STARTS[t] * 2 + yhi * SIZES[t], 32), SIZES[t])

    def piece(t, px, py, c):
        return amp.at[
            amp_rows(t, py >> 1),
            pl.ds(pl.multiple_of(px * 1024 + (py & 1) * 512 + c * 256, 256), 256),
        ]

    def at(u, v, c):
        fx, fy = (u, v) if c == 0 else (v, u)
        return xs[fx], ys[fy]

    def amp_sem(t, px, py, c):
        return amp_recv.at[(t * 16 + place(px, py)) * 2 + c]

    def send(t, src, c, to):
        part = piece(t, *src, c)
        pltpu.make_async_remote_copy(
            part, part, amp_send.at[t], amp_sem(t, *src, c), device_id=device(*to, z, k), device_id_type=MESH
        ).start()

    def arrive(t, src, c):
        wait(piece(t, *src, c), amp_sem(t, *src, c))

    def order(t):
        rows = slice(STARTS[t], STARTS[t] + SIZES[t])
        part = jnp.dot(lhs[rows, :], onehot[...], preferred_element_type=jnp.float32)
        amp[amp_rows(t, yhi_here), pl.ds(pl.multiple_of(block * 512, 512), 512)] = part.astype(jnp.bfloat16)

    def first(t):
        for c in range(2):
            for s in (1, 3):
                send(t, at(0, 0, c), c, at(s, 0, c))

    def spread(t, src, c):
        for s in (1, 3):
            send(t, src, c, at(0, s, c))

    def second(t):
        for c in range(2):
            spread(t, at(0, 0, c), c)
            for s in (1, 3):
                arrive(t, at(s, 0, c), c)
                spread(t, at(s, 0, c), c)
            go = 1 + 2 * ((t + c) % 2)
            send(t, at(4 - go, 0, c), c, at(go, 0, c))

    def third(t):
        for c in range(2):
            arrive(t, at(2, 0, c), c)
            spread(t, at(2, 0, c), c)

    def fourth(t):
        for u in (0, 1, 3, 2):
            for c in range(2):
                go = 1 if u % 2 == 0 else 3
                arrive(t, at(u, 4 - go, c), c)
                send(t, at(u, 4 - go, c), c, at(0, go, c))

    def fifth(t):
        for u in range(4):
            for c in range(2):
                go = 1 if u % 2 == 0 else 3
                arrive(t, at(u, go, c), c)
                arrive(t, at(u, 2, c), c)

    def pair_part(zs, yhi, core):
        return ints.at[pl.ds(pl.multiple_of(((zs * 2 + yhi) * 2 + core) * 256, 256), 256)]

    def pair_out(zs):
        for yhi in range(2):
            pltpu.make_async_remote_copy(
                pair_part(zs, yhi, k), pair_part(zs, yhi, k), pair_send, pair_recv.at[zs * 2 + yhi],
                device_id=device(x, y, z, 1 - k), device_id_type=MESH,
            ).start()

    def pair_in(zs):
        for yhi in range(2):
            wait(pair_part(zs, yhi, 1 - k), pair_recv.at[zs * 2 + yhi])

    sources = [me] + [place(xs[-dx % 4], ys[-dy % 4]) for dx, dy in STEPS]

    def plane_in(parts):
        for p in parts:
            wait(ints.at[pl.ds(ints_row(z, p), 32)], plane_recv.at[p])
            line_copy(z, p, up)
            line_copy(z, p, down)

    lhs[:, pl.ds(pl.multiple_of(k * 256, 256), 256)] = apad[pl.ds(pl.multiple_of(k * HALF, 32), HALF), :]

    @pl.when(holds & fixed)
    def _():
        slots[...] = slot_ref[...]

    @pl.when(jnp.logical_not(holds & fixed))
    def _():
        wait(slots, slot_recv)

    block = col >> 1
    for q in range(4):
        want = jnp.broadcast_to(slots[q : q + 1, :] - block * 512, (128, 128)).T
        for s in range(4):
            place_of = lax.broadcasted_iota(jnp.int32, (128, 128), 1) + s * 128
            stored = ((place_of & 255) >> 5) * 64 + (place_of >> 8) * 32 + (place_of & 31)
            hit = jnp.where(want == stored, 1.0, 0.0).astype(jnp.bfloat16)
            onehot[q * 128 : (q + 1) * 128, s * 128 : (s + 1) * 128] = hit
    half_copy.wait()
    def relay(p):
        src, to = (z + 3 + 2 * (p & 1)) & 3, (z + 1 + 2 * (p & 1)) & 3
        line_wait(src, p)
        line_copy(src, p, to)

    def relays(parts):
        for p in parts:
            relay(p)

    def rest(p, _):
        line_wait((z + 1 + 2 * (p & 1)) & 3, p)
        return _

    def last(p, _):
        line_wait(far, p)
        return _

    def multiply(t):
        size, start = SIZES[t], STARTS[t]

        def one(n, _):
            to = (z + 2 + 3 * n) & 3
            total = jnp.dot(
                amp[2 * start : 2 * (start + size), :],
                ints[:, pl.ds(pl.multiple_of(to * 256, 256), 256)],
                preferred_element_type=jnp.float32,
            )
            for c in range(2):
                for yhi in range(2):
                    part = total[yhi * size : (yhi + 1) * size, c * 128 : (c + 1) * 128]
                    top = jnp.max(jnp.abs(part), axis=0, keepdims=True)
                    scale = TOP / jnp.maximum(top * LIFT, 1e-28)
                    code = jnp.round((part * LIFT) * scale)
                    codes[to * 2 + c, yhi, start : start + size, :] = code.astype(jnp.int32).astype(jnp.int16)
                    tops[to * 2 + c, yhi * 8 + t : yhi * 8 + t + 1, :] = top
                src = codes.at[to * 2 + c, :, pl.ds(start, size)]
                dst = q_ref.at[z, :, pl.ds(pl.multiple_of(k * HALF + start, 32), size)]
                here = (to == z) & (k == c)

                @pl.when(here)
                def _():
                    pltpu.make_async_copy(src, dst, out_recv.at[z * 2 + k]).start()

                @pl.when(jnp.logical_not(here))
                def _():
                    pltpu.make_async_remote_copy(
                        src, dst, out_send.at[t], out_recv.at[z * 2 + k],
                        device_id=device(x, y, to, c), device_id_type=MESH,
                    ).start()

            return _

        lax.fori_loop(0, 4, one, None)

    tops[...] = jnp.zeros_like(tops)

    order(0)
    first(0)
    plane_out(STEPS[8:])
    order(1)
    first(1)
    plane_in(sources[1:8])
    order(2)
    order(3)
    order(4)
    plane_in(sources[8:12])
    second(0)
    plane_in(sources[12:16])
    pair_out(z)
    third(0)
    first(2)
    second(1)
    relays(sources[0:6])
    fourth(0)
    third(1)
    first(3)
    second(2)
    relays(sources[6:16])
    fourth(1)
    lax.fori_loop(0, 16, rest, None)
    pair_out(up)
    pair_out(down)
    third(2)
    first(4)
    second(3)
    lax.fori_loop(0, 16, last, None)
    pair_out(far)
    for zs in range(4):
        pair_in(zs)
    fifth(0)
    multiply(0)
    fourth(2)
    third(3)
    second(4)
    fifth(1)
    multiply(1)
    fourth(3)
    third(4)
    fifth(2)
    multiply(2)
    fourth(4)
    fifth(3)
    multiply(3)
    fifth(4)
    multiply(4)

    for d in range(4):
        for c in range(2):
            to = (z + d) & 3
            src, dst = tops.at[to * 2 + c], m_ref.at[z, k]
            if d:
                pltpu.make_async_remote_copy(
                    src, dst, top_send.at[d * 2 + c], top_recv.at[z * 2 + k],
                    device_id=device(x, y, to, c), device_id_type=MESH,
                ).start()
    other = pltpu.make_async_remote_copy(
        tops.at[z * 2 + 1 - k], m_ref.at[z, k], top_send.at[0], top_recv.at[z * 2 + k],
        device_id=device(x, y, z, 1 - k), device_id_type=MESH,
    )
    other.start()
    pltpu.make_async_copy(tops.at[z * 2 + k], m_ref.at[z, k], top_recv.at[z * 2 + k]).start()

    wait(ipack.at[0:15], plane_send)
    wait(ints.at[0 : 48 * 32], line_send)
    wait(ints.at[0 : 8 * 256], pair_send)
    for t in range(TILES):
        wait(ints.at[0 : 30 * SIZES[t] // 4], amp_send.at[t])
        wait(codes.at[0:7, :, pl.ds(STARTS[t], SIZES[t])], out_send.at[t])

    @pl.when(holds)
    def _():
        for d in range(1, 4):
            slot_copy(d).wait_send()

    @pl.when(holds & jnp.logical_not(fixed))
    def _():
        slot_copy(0).wait_send()

    wait(tops.at[0], top_send.at[0])
    for d in range(1, 4):
        for c in range(2):
            wait(tops.at[0], top_send.at[d * 2 + c])
    for zs in range(4):
        for c in range(2):
            wait(q_ref.at[zs, :, c * HALF : (c + 1) * HALF], out_recv.at[zs * 2 + c])
            wait(m_ref.at[zs, c], top_recv.at[zs * 2 + c])


def decode_kernel(block_rows, q_ref, m_ref, o_ref, values, out_sem):
    outs = []
    for r in range(8):
        lead = r * block_rows % 8
        base, end = r * block_rows - lead, lead + block_rows
        for h in range(2):
            for t in range(TILES):
                start = h * HALF + STARTS[t]
                stop = min(start + SIZES[t], end)
                line = (r % 2) * 8 + t
                top = m_ref[r // 2, h, line : line + 1, :]
                cuts = [max(start, lead), stop]
                if lead and start == 0:
                    cuts.insert(1, 8)
                if stop % 8:
                    cuts.insert(-1, stop // 8 * 8)
                for a, b in zip(cuts, cuts[1:]):
                    code = q_ref[r, a:b, :].astype(jnp.int32).astype(jnp.float32)
                    values[base + a : base + b, :] = (code * (1.0 / TOP)) * top
        low, high = base, (r + 1) * block_rows // 8 * 8
        copy = pltpu.make_async_copy(values.at[low:high], o_ref.at[low:high], out_sem.at[r])
        copy.start()
        outs.append(copy)
    for copy in outs:
        copy.wait()


def shards(amplitudes, integrals, storage_slot):
    dma = pltpu.SemaphoreType.DMA
    bf16 = jnp.bfloat16
    vmem = pl.BlockSpec(memory_space=pltpu.VMEM)
    hbm = pl.BlockSpec(memory_space=pl.ANY)
    codes, tops = pl.pallas_call(
        ladder_kernel,
        out_shape=(
            pltpu.VMEM((4, 2, 2 * HALF, 128), jnp.int16),
            pltpu.VMEM((4, 2, 16, 128), jnp.float32),
        ),
        in_specs=[hbm] * 3,
        out_specs=(vmem, vmem),
        scratch_shapes=[
            pltpu.VMEM(amplitudes.shape, bf16),
            pltpu.VMEM(integrals.shape, bf16),
            pltpu.VMEM((4, 128), jnp.int32),
            dma((3,)),
            pltpu.VMEM((2 * HALF, 256), bf16),
            pltpu.VMEM((HALF, 512), bf16),
            pltpu.VMEM((512, 512), bf16),
            pltpu.VMEM((4, 128), jnp.int32),
            pltpu.VMEM((16, 32, 1024), bf16),
            pltpu.VMEM((2 * HALF, 4096), bf16),
            pltpu.VMEM((4096, 1024), bf16),
            pltpu.VMEM((8, 2, HALF, 128), jnp.int16),
            pltpu.VMEM((8, 16, 128), jnp.float32),
            dma((4,)), dma, dma, dma,
            dma, dma((16,)), dma, dma((64,)), dma, dma((8,)),
            dma((TILES,)), dma((TILES * 32,)), dma((TILES,)), dma((8,)), dma((8,)), dma((8,)),
        ],
        compiler_params=pltpu.CompilerParams(
            collective_id=0, has_side_effects=True, vmem_limit_bytes=57 * 2**20
        ),
    )(amplitudes, integrals, storage_slot.reshape(4, 128))
    rows = amplitudes.shape[0]
    return pl.pallas_call(
        functools.partial(decode_kernel, rows),
        out_shape=jax.ShapeDtypeStruct((8 * rows, 128), jnp.float32),
        in_specs=[vmem, vmem],
        out_specs=hbm,
        scratch_shapes=[
            pltpu.VMEM((8 * rows, 128), jnp.float32),
            dma((8,)),
        ],
        compiler_params=pltpu.CompilerParams(vmem_limit_bytes=32 * 2**20),
    )(codes.reshape(8, 2 * HALF, 128), tops)


def solution(mesh):
    in_specs = (P("row", "col"), P(("row", "col"), None), P("row"))
    out_specs = P(None, ("col", "row"))
    return jax.shard_map(shards, mesh=mesh, in_specs=in_specs, out_specs=out_specs, check_vma=False)
```

```python
import functools

import jax
import jax.numpy as jnp
from jax import lax
from jax.experimental import pallas as pl
from jax.experimental.pallas import tpu as pltpu
from jax.sharding import PartitionSpec as P

MESH = pl.DeviceIdType.MESH
SIZES = (160, 128, 128, 128, 96)
TILES = len(SIZES)
STARTS = tuple(sum(SIZES[:t]) for t in range(TILES))
HALF = sum(SIZES)
LIFT = 2.0**40
TOP = 32767.0
STEPS = (
    (1, 0), (3, 0), (0, 1), (0, 3), (1, 1), (3, 3), (1, 3), (3, 1),
    (2, 0), (0, 2), (2, 1), (2, 3), (1, 2), (3, 2), (2, 2),
)


def device(x, y, z, k):
    return (z * 2 + (y >> 1), x * 4 + (y & 1) * 2 + k)


def wait(ref, sem):
    pltpu.make_async_copy(ref, ref, sem).wait()


def ladder_kernel(
    a_hbm, i_hbm, slot_hbm, q_ref, m_ref,
    a_ref, i_ref, slot_ref, in_sem, apad, lhs, onehot, slots, ipack, amp, ints, codes, tops,
    slot_send, slot_recv, half_send, half_recv,
    plane_send, plane_recv, line_send, line_recv, pair_send, pair_recv,
    amp_send, amp_recv, out_send, out_recv, top_send, top_recv,
):
    row, col = lax.axis_index("row"), lax.axis_index("col")
    x, y, z, k = col >> 2, (row & 1) * 2 + ((col >> 1) & 1), row >> 1, col & 1
    yhi_here = row & 1
    xs, ys = [(x + d) & 3 for d in range(4)], [(y + d) & 3 for d in range(4)]
    me = yhi_here * 8 + (col >> 1)

    def chip_of(p):
        return (p & 7) >> 1, (p >> 3) * 2 + (p & 1)

    def place(px, py):
        return (py >> 1) * 8 + px * 2 + (py & 1)

    loads = [
        pltpu.make_async_copy(src, dst, in_sem.at[i])
        for i, (src, dst) in enumerate(((i_hbm, i_ref), (a_hbm, a_ref), (slot_hbm, slot_ref)))
    ]
    for load in loads:
        load.start()

    barrier = pltpu.get_barrier_semaphore()

    def greet(d):
        pl.semaphore_signal(barrier, inc=1, device_id=d, device_id_type=MESH)

    for dx, dy in reversed(STEPS):
        greet(device(xs[dx], ys[dy], z, k))
    for d in range(1, 4):
        for c in range(2):
            greet(device(x, y, (z + d) & 3, c))
    greet(device(x, y, z, 1 - k))
    turned = (y & 1) * 2 + (y >> 1)
    for d in range(1, 4):
        greet(device(x, turned, (z + d) & 3, k))

    def pack(p, _):
        px, py = chip_of(p)
        base = (px * 2 + (py & 1)) * 16 + (py >> 1)
        for zz in range(4):
            for c in range(2):
                at = pl.multiple_of((base + c * 8 + zz * 2) * 128, 128)
                ipack[p, :, (zz * 2 + c) * 128 : (zz * 2 + c + 1) * 128] = i_ref[:, pl.ds(at, 128)]
        return _

    loads[0].wait()
    lax.fori_loop(0, 16, pack, None)
    rows = a_ref.shape[0]
    low = rows // 16 * 16
    apad[0:16, :] = jnp.zeros((16, 256), jnp.bfloat16)
    apad[low:, :] = jnp.zeros((2 * HALF - low, 256), jnp.bfloat16)
    loads[1].wait()
    for r in range(4):

        @pl.when((row & 3) == r)
        def _():
            lead = rows * r % 8
            apad[lead : lead + rows, :] = a_ref[...]

    loads[2].wait()

    def ints_row(zs, p):
        return pl.multiple_of(((zs * 2 + (p >> 3)) * 2 + k) * 256 + (p & 7) * 32, 32)

    mine = pl.ds(ints_row(z, me), 32)
    ints[mine, :] = ipack[me]

    pl.semaphore_wait(barrier, 25)

    def slot_copy(d):
        return pltpu.make_async_remote_copy(
            slot_ref, slots, slot_send.at[d], slot_recv, device_id=device(x, turned, (z + d) & 3, k), device_id_type=MESH
        )

    holds, fixed = z == x, turned == y

    @pl.when(holds)
    def _():
        for d in range(1, 4):
            slot_copy(d).start()

    @pl.when(holds & jnp.logical_not(fixed))
    def _():
        slot_copy(0).start()

    half_copy = pltpu.make_async_remote_copy(
        apad.at[pl.ds(pl.multiple_of((1 - k) * HALF, 32), HALF)],
        lhs.at[:, pl.ds(pl.multiple_of(k * 256, 256), 256)],
        half_send, half_recv, device_id=device(x, y, z, 1 - k), device_id_type=MESH,
    )
    half_copy.start()

    def line_copy(zs, p, to):
        part = ints.at[pl.ds(ints_row(zs, p), 32)]
        pltpu.make_async_remote_copy(
            part, part, line_send, line_recv.at[zs * 16 + p], device_id=device(x, y, to, k), device_id_type=MESH
        ).start()

    def line_wait(zs, p):
        wait(ints.at[pl.ds(ints_row(zs, p), 32)], line_recv.at[zs * 16 + p])

    up, down, far = (z + 1) & 3, (z + 3) & 3, (z + 2) & 3

    def plane_out(steps):
        for dx, dy in steps:
            px, py = xs[dx], ys[dy]
            pltpu.make_async_remote_copy(
                ipack.at[place(px, py)], ints.at[mine], plane_send, plane_recv.at[me],
                device_id=device(px, py, z, k), device_id_type=MESH,
            ).start()

    plane_out(STEPS)
    line_copy(z, me, up)
    line_copy(z, me, down)

    def amp_rows(t, yhi):
        return pl.ds(pl.multiple_of(STARTS[t] * 2 + yhi * SIZES[t], 32), SIZES[t])

    def piece(t, px, py, c):
        return amp.at[
            amp_rows(t, py >> 1),
            pl.ds(pl.multiple_of(px * 1024 + (py & 1) * 512 + c * 256, 256), 256),
        ]

    def at(u, v, c):
        fx, fy = (u, v) if c == 0 else (v, u)
        return xs[fx], ys[fy]

    def amp_sem(t, px, py, c):
        return amp_recv.at[(t * 16 + place(px, py)) * 2 + c]

    def send(t, src, c, to):
        part = piece(t, *src, c)
        pltpu.make_async_remote_copy(
            part, part, amp_send.at[t], amp_sem(t, *src, c), device_id=device(*to, z, k), device_id_type=MESH
        ).start()

    def arrive(t, src, c):
        wait(piece(t, *src, c), amp_sem(t, *src, c))

    def order(t):
        rows = slice(STARTS[t], STARTS[t] + SIZES[t])
        part = jnp.dot(lhs[rows, :], onehot[...], preferred_element_type=jnp.float32)
        amp[amp_rows(t, yhi_here), pl.ds(pl.multiple_of(block * 512, 512), 512)] = part.astype(jnp.bfloat16)

    def first(t):
        for c in range(2):
            for s in (1, 3):
                send(t, at(0, 0, c), c, at(s, 0, c))

    def spread(t, src, c):
        for s in (1, 3):
            send(t, src, c, at(0, s, c))

    def second(t):
        for c in range(2):
            spread(t, at(0, 0, c), c)
            for s in (1, 3):
                arrive(t, at(s, 0, c), c)
                spread(t, at(s, 0, c), c)
            go = 1 + 2 * ((t + c) % 2)
            send(t, at(4 - go, 0, c), c, at(go, 0, c))

    def third(t):
        for c in range(2):
            arrive(t, at(2, 0, c), c)
            spread(t, at(2, 0, c), c)

    def fourth(t):
        for u in (0, 1, 3, 2):
            for c in range(2):
                go = 1 if u % 2 == 0 else 3
                arrive(t, at(u, 4 - go, c), c)
                send(t, at(u, 4 - go, c), c, at(0, go, c))

    def fifth(t):
        for u in range(4):
            for c in range(2):
                go = 1 if u % 2 == 0 else 3
                arrive(t, at(u, go, c), c)
                arrive(t, at(u, 2, c), c)

    def pair_part(zs, yhi, core):
        return ints.at[pl.ds(pl.multiple_of(((zs * 2 + yhi) * 2 + core) * 256, 256), 256)]

    def pair_out(zs):
        for yhi in range(2):
            pltpu.make_async_remote_copy(
                pair_part(zs, yhi, k), pair_part(zs, yhi, k), pair_send, pair_recv.at[zs * 2 + yhi],
                device_id=device(x, y, z, 1 - k), device_id_type=MESH,
            ).start()

    def pair_in(zs):
        for yhi in range(2):
            wait(pair_part(zs, yhi, 1 - k), pair_recv.at[zs * 2 + yhi])

    sources = [me] + [place(xs[-dx % 4], ys[-dy % 4]) for dx, dy in STEPS]

    def plane_in(parts):
        for p in parts:
            wait(ints.at[pl.ds(ints_row(z, p), 32)], plane_recv.at[p])
            line_copy(z, p, up)
            line_copy(z, p, down)

    lhs[:, pl.ds(pl.multiple_of(k * 256, 256), 256)] = apad[pl.ds(pl.multiple_of(k * HALF, 32), HALF), :]

    @pl.when(holds & fixed)
    def _():
        slots[...] = slot_ref[...]

    @pl.when(jnp.logical_not(holds & fixed))
    def _():
        wait(slots, slot_recv)

    block = col >> 1
    for q in range(4):
        want = jnp.broadcast_to(slots[q : q + 1, :] - block * 512, (128, 128)).T
        for s in range(4):
            place_of = lax.broadcasted_iota(jnp.int32, (128, 128), 1) + s * 128
            stored = ((place_of & 255) >> 5) * 64 + (place_of >> 8) * 32 + (place_of & 31)
            hit = jnp.where(want == stored, 1.0, 0.0).astype(jnp.bfloat16)
            onehot[q * 128 : (q + 1) * 128, s * 128 : (s + 1) * 128] = hit
    half_copy.wait()
    def relay(p):
        src, to = (z + 3 + 2 * (p & 1)) & 3, (z + 1 + 2 * (p & 1)) & 3
        line_wait(src, p)
        line_copy(src, p, to)

    def relays(parts):
        for p in parts:
            relay(p)

    def rest(p, _):
        line_wait((z + 1 + 2 * (p & 1)) & 3, p)
        return _

    def last(p, _):
        line_wait(far, p)
        return _

    def multiply(t):
        size, start = SIZES[t], STARTS[t]

        def one(n, _):
            to = (z + 2 + 3 * n) & 3
            total = jnp.dot(
                amp[2 * start : 2 * (start + size), :],
                ints[:, pl.ds(pl.multiple_of(to * 256, 256), 256)],
                preferred_element_type=jnp.float32,
            )
            for c in range(2):
                for yhi in range(2):
                    part = total[yhi * size : (yhi + 1) * size, c * 128 : (c + 1) * 128]
                    top = jnp.max(jnp.abs(part), axis=0, keepdims=True)
                    scale = TOP / jnp.maximum(top * LIFT, 1e-28)
                    code = jnp.round((part * LIFT) * scale)
                    codes[to * 2 + c, yhi, start : start + size, :] = code.astype(jnp.int32).astype(jnp.int16)
                    tops[to * 2 + c, yhi * 8 + t : yhi * 8 + t + 1, :] = top
                src = codes.at[to * 2 + c, :, pl.ds(start, size)]
                dst = q_ref.at[z, :, pl.ds(pl.multiple_of(k * HALF + start, 32), size)]
                here = (to == z) & (k == c)

                @pl.when(here)
                def _():
                    pltpu.make_async_copy(src, dst, out_recv.at[z * 2 + k]).start()

                @pl.when(jnp.logical_not(here))
                def _():
                    pltpu.make_async_remote_copy(
                        src, dst, out_send.at[t], out_recv.at[z * 2 + k],
                        device_id=device(x, y, to, c), device_id_type=MESH,
                    ).start()

            return _

        lax.fori_loop(0, 4, one, None)

    tops[...] = jnp.zeros_like(tops)

    order(0)
    first(0)
    order(1)
    first(1)
    plane_in(sources[1:8])
    order(2)
    order(3)
    order(4)
    plane_in(sources[8:12])
    second(0)
    plane_in(sources[12:16])
    pair_out(z)
    third(0)
    first(2)
    second(1)
    relays(sources[0:6])
    fourth(0)
    third(1)
    first(3)
    second(2)
    relays(sources[6:16])
    fourth(1)
    lax.fori_loop(0, 16, rest, None)
    pair_out(up)
    pair_out(down)
    third(2)
    second(3)
    first(4)
    lax.fori_loop(0, 16, last, None)
    pair_out(far)
    for zs in range(4):
        pair_in(zs)
    fifth(0)
    multiply(0)
    fourth(2)
    third(3)
    second(4)
    fifth(1)
    multiply(1)
    fourth(3)
    third(4)
    fifth(2)
    multiply(2)
    fourth(4)
    fifth(3)
    multiply(3)
    fifth(4)
    multiply(4)

    for d in range(4):
        for c in range(2):
            to = (z + d) & 3
            src, dst = tops.at[to * 2 + c], m_ref.at[z, k]
            if d:
                pltpu.make_async_remote_copy(
                    src, dst, top_send.at[d * 2 + c], top_recv.at[z * 2 + k],
                    device_id=device(x, y, to, c), device_id_type=MESH,
                ).start()
    other = pltpu.make_async_remote_copy(
        tops.at[z * 2 + 1 - k], m_ref.at[z, k], top_send.at[0], top_recv.at[z * 2 + k],
        device_id=device(x, y, z, 1 - k), device_id_type=MESH,
    )
    other.start()
    pltpu.make_async_copy(tops.at[z * 2 + k], m_ref.at[z, k], top_recv.at[z * 2 + k]).start()

    wait(ipack.at[0:15], plane_send)
    wait(ints.at[0 : 48 * 32], line_send)
    wait(ints.at[0 : 8 * 256], pair_send)
    for t in range(TILES):
        wait(ints.at[0 : 30 * SIZES[t] // 4], amp_send.at[t])
        wait(codes.at[0:7, :, pl.ds(STARTS[t], SIZES[t])], out_send.at[t])

    @pl.when(holds)
    def _():
        for d in range(1, 4):
            slot_copy(d).wait_send()

    @pl.when(holds & jnp.logical_not(fixed))
    def _():
        slot_copy(0).wait_send()

    wait(tops.at[0], top_send.at[0])
    for d in range(1, 4):
        for c in range(2):
            wait(tops.at[0], top_send.at[d * 2 + c])
    for zs in range(4):
        for c in range(2):
            wait(q_ref.at[zs, :, c * HALF : (c + 1) * HALF], out_recv.at[zs * 2 + c])
            wait(m_ref.at[zs, c], top_recv.at[zs * 2 + c])


def decode_kernel(block_rows, q_ref, m_ref, o_ref, values, out_sem):
    outs = []
    for r in range(8):
        lead = r * block_rows % 8
        base, end = r * block_rows - lead, lead + block_rows
        for h in range(2):
            for t in range(TILES):
                start = h * HALF + STARTS[t]
                stop = min(start + SIZES[t], end)
                line = (r % 2) * 8 + t
                top = m_ref[r // 2, h, line : line + 1, :]
                cuts = [max(start, lead), stop]
                if lead and start == 0:
                    cuts.insert(1, 8)
                if stop % 8:
                    cuts.insert(-1, stop // 8 * 8)
                for a, b in zip(cuts, cuts[1:]):
                    code = q_ref[r, a:b, :].astype(jnp.int32).astype(jnp.float32)
                    values[base + a : base + b, :] = (code * (1.0 / TOP)) * top
        low, high = base, (r + 1) * block_rows // 8 * 8
        copy = pltpu.make_async_copy(values.at[low:high], o_ref.at[low:high], out_sem.at[r])
        copy.start()
        outs.append(copy)
    for copy in outs:
        copy.wait()


def shards(amplitudes, integrals, storage_slot):
    dma = pltpu.SemaphoreType.DMA
    bf16 = jnp.bfloat16
    vmem = pl.BlockSpec(memory_space=pltpu.VMEM)
    hbm = pl.BlockSpec(memory_space=pl.ANY)
    codes, tops = pl.pallas_call(
        ladder_kernel,
        out_shape=(
            pltpu.VMEM((4, 2, 2 * HALF, 128), jnp.int16),
            pltpu.VMEM((4, 2, 16, 128), jnp.float32),
        ),
        in_specs=[hbm] * 3,
        out_specs=(vmem, vmem),
        scratch_shapes=[
            pltpu.VMEM(amplitudes.shape, bf16),
            pltpu.VMEM(integrals.shape, bf16),
            pltpu.VMEM((4, 128), jnp.int32),
            dma((3,)),
            pltpu.VMEM((2 * HALF, 256), bf16),
            pltpu.VMEM((HALF, 512), bf16),
            pltpu.VMEM((512, 512), bf16),
            pltpu.VMEM((4, 128), jnp.int32),
            pltpu.VMEM((16, 32, 1024), bf16),
            pltpu.VMEM((2 * HALF, 4096), bf16),
            pltpu.VMEM((4096, 1024), bf16),
            pltpu.VMEM((8, 2, HALF, 128), jnp.int16),
            pltpu.VMEM((8, 16, 128), jnp.float32),
            dma((4,)), dma, dma, dma,
            dma, dma((16,)), dma, dma((64,)), dma, dma((8,)),
            dma((TILES,)), dma((TILES * 32,)), dma((TILES,)), dma((8,)), dma((8,)), dma((8,)),
        ],
        compiler_params=pltpu.CompilerParams(
            collective_id=0, has_side_effects=True, vmem_limit_bytes=57 * 2**20
        ),
    )(amplitudes, integrals, storage_slot.reshape(4, 128))
    rows = amplitudes.shape[0]
    return pl.pallas_call(
        functools.partial(decode_kernel, rows),
        out_shape=jax.ShapeDtypeStruct((8 * rows, 128), jnp.float32),
        in_specs=[vmem, vmem],
        out_specs=hbm,
        scratch_shapes=[
            pltpu.VMEM((8 * rows, 128), jnp.float32),
            dma((8,)),
        ],
        compiler_params=pltpu.CompilerParams(vmem_limit_bytes=32 * 2**20),
    )(codes.reshape(8, 2 * HALF, 128), tops)


def solution(mesh):
    in_specs = (P("row", "col"), P(("row", "col"), None), P("row"))
    out_specs = P(None, ("col", "row"))
    return jax.shard_map(shards, mesh=mesh, in_specs=in_specs, out_specs=out_specs, check_vma=False)
```

```python
import functools

import jax
import jax.numpy as jnp
from jax import lax
from jax.experimental import pallas as pl
from jax.experimental.pallas import tpu as pltpu
from jax.sharding import PartitionSpec as P

MESH = pl.DeviceIdType.MESH
SIZES = (160, 128, 128, 128, 96)
TILES = len(SIZES)
STARTS = tuple(sum(SIZES[:t]) for t in range(TILES))
HALF = sum(SIZES)
LIFT = 2.0**40
TOP = 32767.0
STEPS = (
    (1, 0), (3, 0), (0, 1), (0, 3), (1, 1), (3, 3), (1, 3), (3, 1),
    (2, 0), (0, 2), (2, 1), (2, 3), (1, 2), (3, 2), (2, 2),
)


def device(x, y, z, k):
    return (z * 2 + (y >> 1), x * 4 + (y & 1) * 2 + k)


def wait(ref, sem):
    pltpu.make_async_copy(ref, ref, sem).wait()


def ladder_kernel(
    a_hbm, i_hbm, slot_hbm, q_ref, m_ref,
    a_ref, i_ref, slot_ref, in_sem, apad, lhs, onehot, slots, ipack, amp, ints, codes, tops,
    slot_send, slot_recv, half_send, half_recv,
    plane_send, plane_recv, line_send, line_recv, pair_send, pair_recv,
    amp_send, amp_recv, out_send, out_recv, top_send, top_recv,
):
    row, col = lax.axis_index("row"), lax.axis_index("col")
    x, y, z, k = col >> 2, (row & 1) * 2 + ((col >> 1) & 1), row >> 1, col & 1
    yhi_here = row & 1
    xs, ys = [(x + d) & 3 for d in range(4)], [(y + d) & 3 for d in range(4)]
    me = yhi_here * 8 + (col >> 1)

    def chip_of(p):
        return (p & 7) >> 1, (p >> 3) * 2 + (p & 1)

    def place(px, py):
        return (py >> 1) * 8 + px * 2 + (py & 1)

    loads = [
        pltpu.make_async_copy(src, dst, in_sem.at[i])
        for i, (src, dst) in enumerate(((i_hbm, i_ref), (a_hbm, a_ref), (slot_hbm, slot_ref)))
    ]
    for load in loads:
        load.start()

    barrier = pltpu.get_barrier_semaphore()

    def greet(d):
        pl.semaphore_signal(barrier, inc=1, device_id=d, device_id_type=MESH)

    for dx, dy in reversed(STEPS):
        greet(device(xs[dx], ys[dy], z, k))
    for d in range(1, 4):
        for c in range(2):
            greet(device(x, y, (z + d) & 3, c))
    greet(device(x, y, z, 1 - k))
    turned = (y & 1) * 2 + (y >> 1)
    for d in range(1, 4):
        greet(device(x, turned, (z + d) & 3, k))

    def pack(p, _):
        px, py = chip_of(p)
        base = (px * 2 + (py & 1)) * 16 + (py >> 1)
        for zz in range(4):
            for c in range(2):
                at = pl.multiple_of((base + c * 8 + zz * 2) * 128, 128)
                ipack[p, :, (zz * 2 + c) * 128 : (zz * 2 + c + 1) * 128] = i_ref[:, pl.ds(at, 128)]
        return _

    loads[0].wait()
    lax.fori_loop(0, 16, pack, None)
    rows = a_ref.shape[0]
    low = rows // 16 * 16
    apad[0:16, :] = jnp.zeros((16, 256), jnp.bfloat16)
    apad[low:, :] = jnp.zeros((2 * HALF - low, 256), jnp.bfloat16)
    loads[1].wait()
    for r in range(4):

        @pl.when((row & 3) == r)
        def _():
            lead = rows * r % 8
            apad[lead : lead + rows, :] = a_ref[...]

    loads[2].wait()

    def ints_row(zs, p):
        return pl.multiple_of(((zs * 2 + (p >> 3)) * 2 + k) * 256 + (p & 7) * 32, 32)

    mine = pl.ds(ints_row(z, me), 32)
    ints[mine, :] = ipack[me]

    pl.semaphore_wait(barrier, 25)

    def slot_copy(d):
        return pltpu.make_async_remote_copy(
            slot_ref, slots, slot_send.at[d], slot_recv, device_id=device(x, turned, (z + d) & 3, k), device_id_type=MESH
        )

    holds, fixed = z == x, turned == y

    @pl.when(holds)
    def _():
        for d in range(1, 4):
            slot_copy(d).start()

    @pl.when(holds & jnp.logical_not(fixed))
    def _():
        slot_copy(0).start()

    half_copy = pltpu.make_async_remote_copy(
        apad.at[pl.ds(pl.multiple_of((1 - k) * HALF, 32), HALF)],
        lhs.at[:, pl.ds(pl.multiple_of(k * 256, 256), 256)],
        half_send, half_recv, device_id=device(x, y, z, 1 - k), device_id_type=MESH,
    )
    half_copy.start()

    def line_copy(zs, p, to):
        part = ints.at[pl.ds(ints_row(zs, p), 32)]
        pltpu.make_async_remote_copy(
            part, part, line_send, line_recv.at[zs * 16 + p], device_id=device(x, y, to, k), device_id_type=MESH
        ).start()

    def line_wait(zs, p):
        wait(ints.at[pl.ds(ints_row(zs, p), 32)], line_recv.at[zs * 16 + p])

    up, down, far = (z + 1) & 3, (z + 3) & 3, (z + 2) & 3

    def plane_out(steps):
        for dx, dy in steps:
            px, py = xs[dx], ys[dy]
            pltpu.make_async_remote_copy(
                ipack.at[place(px, py)], ints.at[mine], plane_send, plane_recv.at[me],
                device_id=device(px, py, z, k), device_id_type=MESH,
            ).start()

    plane_out(STEPS)
    line_copy(z, me, up)
    line_copy(z, me, down)

    def amp_rows(t, yhi):
        return pl.ds(pl.multiple_of(STARTS[t] * 2 + yhi * SIZES[t], 32), SIZES[t])

    def piece(t, px, py, c):
        return amp.at[
            amp_rows(t, py >> 1),
            pl.ds(pl.multiple_of(px * 1024 + (py & 1) * 512 + c * 256, 256), 256),
        ]

    def at(u, v, c):
        fx, fy = (u, v) if c == 0 else (v, u)
        return xs[fx], ys[fy]

    def amp_sem(t, px, py, c):
        return amp_recv.at[(t * 16 + place(px, py)) * 2 + c]

    def send(t, src, c, to):
        part = piece(t, *src, c)
        pltpu.make_async_remote_copy(
            part, part, amp_send.at[t], amp_sem(t, *src, c), device_id=device(*to, z, k), device_id_type=MESH
        ).start()

    def arrive(t, src, c):
        wait(piece(t, *src, c), amp_sem(t, *src, c))

    def order(t):
        rows = slice(STARTS[t], STARTS[t] + SIZES[t])
        part = jnp.dot(lhs[rows, :], onehot[...], preferred_element_type=jnp.float32)
        amp[amp_rows(t, yhi_here), pl.ds(pl.multiple_of(block * 512, 512), 512)] = part.astype(jnp.bfloat16)

    def first(t):
        for c in range(2):
            for s in (1, 3):
                send(t, at(0, 0, c), c, at(s, 0, c))

    def spread(t, src, c):
        for s in (1, 3):
            send(t, src, c, at(0, s, c))

    def second(t):
        for c in range(2):
            spread(t, at(0, 0, c), c)
            for s in (1, 3):
                arrive(t, at(s, 0, c), c)
                spread(t, at(s, 0, c), c)
            go = 1 + 2 * ((t + c) % 2)
            send(t, at(4 - go, 0, c), c, at(go, 0, c))

    def third(t):
        for c in range(2):
            arrive(t, at(2, 0, c), c)
            spread(t, at(2, 0, c), c)

    def fourth(t):
        for u in (0, 1, 3, 2):
            for c in range(2):
                go = 1 if u % 2 == 0 else 3
                arrive(t, at(u, 4 - go, c), c)
                send(t, at(u, 4 - go, c), c, at(0, go, c))

    def fifth(t):
        for u in range(4):
            for c in range(2):
                go = 1 if u % 2 == 0 else 3
                arrive(t, at(u, go, c), c)
                arrive(t, at(u, 2, c), c)

    def pair_part(zs, yhi, core):
        return ints.at[pl.ds(pl.multiple_of(((zs * 2 + yhi) * 2 + core) * 256, 256), 256)]

    def pair_out(zs):
        for yhi in range(2):
            pltpu.make_async_remote_copy(
                pair_part(zs, yhi, k), pair_part(zs, yhi, k), pair_send, pair_recv.at[zs * 2 + yhi],
                device_id=device(x, y, z, 1 - k), device_id_type=MESH,
            ).start()

    def pair_in(zs):
        for yhi in range(2):
            wait(pair_part(zs, yhi, 1 - k), pair_recv.at[zs * 2 + yhi])

    sources = [me] + [place(xs[-dx % 4], ys[-dy % 4]) for dx, dy in STEPS]

    def plane_in(parts):
        for p in parts:
            wait(ints.at[pl.ds(ints_row(z, p), 32)], plane_recv.at[p])
            line_copy(z, p, up)
            line_copy(z, p, down)

    lhs[:, pl.ds(pl.multiple_of(k * 256, 256), 256)] = apad[pl.ds(pl.multiple_of(k * HALF, 32), HALF), :]

    @pl.when(holds & fixed)
    def _():
        slots[...] = slot_ref[...]

    @pl.when(jnp.logical_not(holds & fixed))
    def _():
        wait(slots, slot_recv)

    block = col >> 1
    for q in range(4):
        want = jnp.broadcast_to(slots[q : q + 1, :] - block * 512, (128, 128)).T
        for s in range(4):
            place_of = lax.broadcasted_iota(jnp.int32, (128, 128), 1) + s * 128
            stored = ((place_of & 255) >> 5) * 64 + (place_of >> 8) * 32 + (place_of & 31)
            hit = jnp.where(want == stored, 1.0, 0.0).astype(jnp.bfloat16)
            onehot[q * 128 : (q + 1) * 128, s * 128 : (s + 1) * 128] = hit
    half_copy.wait()
    def relay(p):
        src, to = (z + 3 + 2 * (p & 1)) & 3, (z + 1 + 2 * (p & 1)) & 3
        line_wait(src, p)
        line_copy(src, p, to)

    def relays(parts):
        for p in parts:
            relay(p)

    def rest(p, _):
        line_wait((z + 1 + 2 * (p & 1)) & 3, p)
        return _

    def last(p, _):
        line_wait(far, p)
        return _

    def multiply(t):
        size, start = SIZES[t], STARTS[t]

        def one(n, _):
            to = (z + 2 + 3 * n + (n >> 1) * (3 - 2 * (n & 1))) & 3
            total = jnp.dot(
                amp[2 * start : 2 * (start + size), :],
                ints[:, pl.ds(pl.multiple_of(to * 256, 256), 256)],
                preferred_element_type=jnp.float32,
            )
            for c in range(2):
                for yhi in range(2):
                    part = total[yhi * size : (yhi + 1) * size, c * 128 : (c + 1) * 128]
                    top = jnp.max(jnp.abs(part), axis=0, keepdims=True)
                    scale = TOP / jnp.maximum(top * LIFT, 1e-28)
                    code = jnp.round((part * LIFT) * scale)
                    codes[to * 2 + c, yhi, start : start + size, :] = code.astype(jnp.int32).astype(jnp.int16)
                    tops[to * 2 + c, yhi * 8 + t : yhi * 8 + t + 1, :] = top
                src = codes.at[to * 2 + c, :, pl.ds(start, size)]
                dst = q_ref.at[z, :, pl.ds(pl.multiple_of(k * HALF + start, 32), size)]
                here = (to == z) & (k == c)

                @pl.when(here)
                def _():
                    pltpu.make_async_copy(src, dst, out_recv.at[z * 2 + k]).start()

                @pl.when(jnp.logical_not(here))
                def _():
                    pltpu.make_async_remote_copy(
                        src, dst, out_send.at[t], out_recv.at[z * 2 + k],
                        device_id=device(x, y, to, c), device_id_type=MESH,
                    ).start()

            return _

        lax.fori_loop(0, 4, one, None)

    tops[...] = jnp.zeros_like(tops)

    order(0)
    first(0)
    order(1)
    first(1)
    plane_in(sources[1:8])
    order(2)
    order(3)
    order(4)
    plane_in(sources[8:12])
    second(0)
    plane_in(sources[12:16])
    pair_out(z)
    third(0)
    first(2)
    second(1)
    relays(sources[0:6])
    fourth(0)
    third(1)
    first(3)
    second(2)
    relays(sources[6:16])
    fourth(1)
    lax.fori_loop(0, 16, rest, None)
    pair_out(up)
    pair_out(down)
    third(2)
    second(3)
    first(4)
    lax.fori_loop(0, 16, last, None)
    pair_out(far)
    for zs in range(4):
        pair_in(zs)
    fifth(0)
    multiply(0)
    fourth(2)
    third(3)
    second(4)
    fifth(1)
    multiply(1)
    fourth(3)
    third(4)
    fifth(2)
    multiply(2)
    fourth(4)
    fifth(3)
    multiply(3)
    fifth(4)
    multiply(4)

    for d in range(4):
        for c in range(2):
            to = (z + d) & 3
            src, dst = tops.at[to * 2 + c], m_ref.at[z, k]
            if d:
                pltpu.make_async_remote_copy(
                    src, dst, top_send.at[d * 2 + c], top_recv.at[z * 2 + k],
                    device_id=device(x, y, to, c), device_id_type=MESH,
                ).start()
    other = pltpu.make_async_remote_copy(
        tops.at[z * 2 + 1 - k], m_ref.at[z, k], top_send.at[0], top_recv.at[z * 2 + k],
        device_id=device(x, y, z, 1 - k), device_id_type=MESH,
    )
    other.start()
    pltpu.make_async_copy(tops.at[z * 2 + k], m_ref.at[z, k], top_recv.at[z * 2 + k]).start()

    wait(ipack.at[0:15], plane_send)
    wait(ints.at[0 : 48 * 32], line_send)
    wait(ints.at[0 : 8 * 256], pair_send)
    for t in range(TILES):
        wait(ints.at[0 : 30 * SIZES[t] // 4], amp_send.at[t])
        wait(codes.at[0:7, :, pl.ds(STARTS[t], SIZES[t])], out_send.at[t])

    @pl.when(holds)
    def _():
        for d in range(1, 4):
            slot_copy(d).wait_send()

    @pl.when(holds & jnp.logical_not(fixed))
    def _():
        slot_copy(0).wait_send()

    wait(tops.at[0], top_send.at[0])
    for d in range(1, 4):
        for c in range(2):
            wait(tops.at[0], top_send.at[d * 2 + c])
    for zs in range(4):
        for c in range(2):
            wait(q_ref.at[zs, :, c * HALF : (c + 1) * HALF], out_recv.at[zs * 2 + c])
            wait(m_ref.at[zs, c], top_recv.at[zs * 2 + c])


def decode_kernel(block_rows, q_ref, m_ref, o_ref, values, out_sem):
    outs = []
    for r in range(8):
        lead = r * block_rows % 8
        base, end = r * block_rows - lead, lead + block_rows
        for h in range(2):
            for t in range(TILES):
                start = h * HALF + STARTS[t]
                stop = min(start + SIZES[t], end)
                line = (r % 2) * 8 + t
                top = m_ref[r // 2, h, line : line + 1, :]
                cuts = [max(start, lead), stop]
                if lead and start == 0:
                    cuts.insert(1, 8)
                if stop % 8:
                    cuts.insert(-1, stop // 8 * 8)
                for a, b in zip(cuts, cuts[1:]):
                    code = q_ref[r, a:b, :].astype(jnp.int32).astype(jnp.float32)
                    values[base + a : base + b, :] = (code * (1.0 / TOP)) * top
        low, high = base, (r + 1) * block_rows // 8 * 8
        copy = pltpu.make_async_copy(values.at[low:high], o_ref.at[low:high], out_sem.at[r])
        copy.start()
        outs.append(copy)
    for copy in outs:
        copy.wait()


def shards(amplitudes, integrals, storage_slot):
    dma = pltpu.SemaphoreType.DMA
    bf16 = jnp.bfloat16
    vmem = pl.BlockSpec(memory_space=pltpu.VMEM)
    hbm = pl.BlockSpec(memory_space=pl.ANY)
    codes, tops = pl.pallas_call(
        ladder_kernel,
        out_shape=(
            pltpu.VMEM((4, 2, 2 * HALF, 128), jnp.int16),
            pltpu.VMEM((4, 2, 16, 128), jnp.float32),
        ),
        in_specs=[hbm] * 3,
        out_specs=(vmem, vmem),
        scratch_shapes=[
            pltpu.VMEM(amplitudes.shape, bf16),
            pltpu.VMEM(integrals.shape, bf16),
            pltpu.VMEM((4, 128), jnp.int32),
            dma((3,)),
            pltpu.VMEM((2 * HALF, 256), bf16),
            pltpu.VMEM((HALF, 512), bf16),
            pltpu.VMEM((512, 512), bf16),
            pltpu.VMEM((4, 128), jnp.int32),
            pltpu.VMEM((16, 32, 1024), bf16),
            pltpu.VMEM((2 * HALF, 4096), bf16),
            pltpu.VMEM((4096, 1024), bf16),
            pltpu.VMEM((8, 2, HALF, 128), jnp.int16),
            pltpu.VMEM((8, 16, 128), jnp.float32),
            dma((4,)), dma, dma, dma,
            dma, dma((16,)), dma, dma((64,)), dma, dma((8,)),
            dma((TILES,)), dma((TILES * 32,)), dma((TILES,)), dma((8,)), dma((8,)), dma((8,)),
        ],
        compiler_params=pltpu.CompilerParams(
            collective_id=0, has_side_effects=True, vmem_limit_bytes=57 * 2**20
        ),
    )(amplitudes, integrals, storage_slot.reshape(4, 128))
    rows = amplitudes.shape[0]
    return pl.pallas_call(
        functools.partial(decode_kernel, rows),
        out_shape=jax.ShapeDtypeStruct((8 * rows, 128), jnp.float32),
        in_specs=[vmem, vmem],
        out_specs=hbm,
        scratch_shapes=[
            pltpu.VMEM((8 * rows, 128), jnp.float32),
            dma((8,)),
        ],
        compiler_params=pltpu.CompilerParams(vmem_limit_bytes=32 * 2**20),
    )(codes.reshape(8, 2 * HALF, 128), tops)


def solution(mesh):
    in_specs = (P("row", "col"), P(("row", "col"), None), P("row"))
    out_specs = P(None, ("col", "row"))
    return jax.shard_map(shards, mesh=mesh, in_specs=in_specs, out_specs=out_specs, check_vma=False)
```
